128 devices in a mesh: dp: 8 (over x, z_hi), tensor: 16 (over y, z_lo, core).
Axes of the slice: x: 4, y: 4, z: 4 (z_hi: 2, z_lo: 2; z = z_hi * 2 + z_lo), core: 2. Of those that a mesh axis runs over, the one named last changes fastest.
Arguments:
- out_grads: bfloat16 [32768, 4096], P('dp', 'tensor'), may hold values from -6 to 6
- inputs: bfloat16 [32768, 1024], P('dp', 'tensor'), may hold values from -6 to 6
- out_proj: bfloat16 [4096, 2048], P('tensor'), may hold values from -0.09375 to 0.09375
- in_proj: bfloat16 [1024, 2048], P('tensor'), may hold values from -0.1875 to 0.1875
- prev_gram: float32 [2048, 2048], P('tensor'), may hold values from -3 to 3
Outputs:
- features: float32 [64, 2048], P('dp', 'tensor')
- gram: float32 [2048, 2048], P('tensor')
The draws below stay inside these ranges and needn't reach their ends.
All inputs are finite; a program needn't handle non-finite values.
Results may differ from the reference program's by a relative error of at most 0.0003.
Values may be sent and summed in bfloat16 or wider, within the bound.
A program may use at most 256 MiB of HBM per device.

```python
import math
import jax
import jax.numpy as jnp
from jax import lax

D = 1024
FF = 4096
K = 2048
SEQ = 512
ALL_CLIPS = 64


def block_levels(stream_key, dims, cuts, smallest, high):
    gain = 1.0
    for axis_at, parts in cuts:
        heights = jax.random.uniform(jax.random.fold_in(jax.random.fold_in(stream_key, 6), axis_at), (parts,), jnp.float32, smallest / len(cuts), high / len(cuts))
        gain = gain * jnp.repeat(jnp.exp(heights), dims[axis_at] // parts).reshape((-1,) + (1,) * (len(dims) - 1 - axis_at))
    return gain


def centred(key, shape, spread, limit, pieces=(), kind=jnp.bfloat16):
    result = jax.random.normal(key, shape, jnp.float32) * spread
    if len(pieces) > 0:
        result = block_levels(key, shape, pieces, -0.22, 0.18) * result
    return jnp.clip(result, min=-limit, max=limit).astype(kind)


def setup_inputs(seed: int = 0) -> dict:
    seeds = jax.random.split(jax.random.key(seed), 6)
    return {
        "out_grads": centred(seeds[0], (ALL_CLIPS * SEQ, FF), 1.0, 6.0, ((0, 8), (1, 16))),
        "inputs": centred(seeds[1], (ALL_CLIPS * SEQ, D), 1.0, 6.0, ((0, 8), (1, 16))),
        "out_proj": centred(seeds[2], (FF, K), FF ** -0.5, 0.09375, ((0, 16),)),
        "in_proj": centred(seeds[3], (D, K), D ** -0.5, 0.1875, ((0, 16),)),
        "prev_gram": centred(seeds[4], (K, K), 0.5, 3.0, ((0, 16),), jnp.float32),
    }


def reference(out_grads, inputs, out_proj, in_proj, prev_gram):
    row_count = out_grads.shape[0]
    out_side = jnp.dot(out_grads, out_proj, preferred_element_type=jnp.float32)
    in_side = jnp.dot(inputs, in_proj, preferred_element_type=jnp.float32)
    products = (out_side * in_side).reshape(row_count // SEQ, SEQ, K)
    features = lax.optimization_barrier(jnp.sum(products, axis=1)) * jnp.float32(1.0 / math.sqrt(SEQ))
    gram_part = jnp.dot(features.T, features, precision=lax.Precision.HIGHEST, preferred_element_type=jnp.float32)
    gram = prev_gram + gram_part / jnp.float32(row_count // SEQ)
    return (features, gram)
```

```python
import math

import jax
import jax.numpy as jnp
from jax import lax
from jax.sharding import PartitionSpec as P

SEQ = 512


def local(out_grads, inputs, out_proj, in_proj, prev_gram):
    row_count = out_grads.shape[0]
    clip_count = row_count // SEQ
    width = out_proj.shape[1]
    norm_scale = jnp.float32(1.0 / math.sqrt(SEQ))
    all_inputs = lax.all_gather(inputs, "tensor", axis=1, tiled=True)
    all_in_proj = lax.all_gather(in_proj, "tensor", axis=0, tiled=True)
    out_part = jnp.dot(out_grads, out_proj, preferred_element_type=jnp.float32)
    in_side = jnp.dot(all_inputs, all_in_proj, preferred_element_type=jnp.float32)
    partial_features = jnp.sum((out_part * in_side).reshape(clip_count, SEQ, width), axis=1)
    own = lax.psum_scatter(partial_features, "tensor", scatter_dimension=1, tiled=True) * norm_scale
    own_columns = lax.all_gather(own, "dp", axis=0, tiled=True)
    features = lax.all_gather(own_columns, "tensor", axis=1, tiled=True)
    gram_part = jnp.dot(
        own_columns.T,
        features,
        precision=lax.Precision.HIGHEST,
        preferred_element_type=jnp.float32,
    )
    gram = prev_gram + gram_part / jnp.float32(clip_count * lax.axis_size("dp"))
    return (own, gram)


def solution(mesh):
    return jax.shard_map(
        local,
        mesh=mesh,
        in_specs=(
            P("dp", "tensor"),
            P("dp", "tensor"),
            P("tensor", None),
            P("tensor", None),
            P("tensor", None),
        ),
        out_specs=(P("dp", "tensor"), P("tensor", None)),
        check_vma=False,
    )
```

```python
import functools
import math

import jax
import jax.numpy as jnp
from jax import lax
from jax.experimental import pallas as pl
from jax.experimental.pallas import tpu as pltpu
from jax.sharding import PartitionSpec as P

SEQ = 512
NI = 4
NJ = 4
F32 = jnp.float32
BF16 = jnp.bfloat16


def kernel(
    og, inp, op, ip, prev, feat_out, gram_out,
    X, Y, Wo, Wi, own_in, par_in, pz, part, r1buf, fall, lsem, ssem, rsem,
):
    dp = lax.axis_index("dp")
    t = lax.axis_index("tensor")
    x, zh = dp // 2, dp % 2
    y, zl, c = t // 4, (t // 2) % 2, t % 2
    tok = og.shape[0] // 4
    width = op.shape[1]
    ti, wj = tok // NI, width // NJ

    def dev(x_, zh_, y_, zl_, c_):
        return (x_ * 2 + zh_, (y_ * 2 + zl_) * 2 + c_)

    partner = dev(x, zh, y, zl, 1 - c)
    zlo = dev(x, zh, y, 1 - zl, c)
    zlo_other = dev(x, zh, y, 1 - zl, 1 - c)
    zhi = dev(x, 1 - zh, y, 1 - zl, c)
    ypeer = [dev(x, zh, (y + d) % 4, zl, c) for d in (1, 3, 2)]
    xpeer = [dev((x + d) % 4, zh, y, zl, c) for d in (1, 3, 2)]
    tpeer = [(dp, (t + d) % 16) for d in range(1, 16)]
    dpeer = [((dp + d) % 8, t) for d in range(1, 8)]

    copies = []

    def send(src, dst, device):
        k = len(copies)
        cp = pltpu.make_async_remote_copy(
            src_ref=src, dst_ref=dst, send_sem=ssem.at[k], recv_sem=rsem.at[k],
            device_id=device, device_id_type=pl.DeviceIdType.MESH,
        )
        cp.start()
        copies.append(cp)
        return cp

    locals_ = []

    def local(src, dst):
        cp = pltpu.make_async_copy(src, dst, lsem.at[len(locals_)])
        cp.start()
        locals_.append(cp)
        return cp

    blk = zl * 2 + c
    oblk = (1 - zl) * 2 + c

    def rows(b, i=0, n=tok):
        return pl.ds(pl.multiple_of(b * tok + i * n, 256), n)

    def xcol(b):
        return pl.ds(pl.multiple_of(b * 256, 256), 256)

    def ycol(p):
        return pl.ds(pl.multiple_of(p * 128, 128), 128)

    l_in = [local(inp.at[rows(k * 2 + c)], own_in.at[k]) for k in range(2)]
    l_wi = local(ip.at[x], Wi.at[y, zl, c, x])
    l_x = local(og.at[rows(blk)], X.at[:, xcol(blk)])
    l_wo = local(op, Wo.at[xcol(blk)])
    part[...] = jnp.zeros_like(part)

    bar = pltpu.get_barrier_semaphore()
    peers = tpeer + dpeer + [zhi]
    for d in peers:
        pl.semaphore_signal(bar, inc=1, device_id=d, device_id_type=pl.DeviceIdType.MESH)
    pl.semaphore_wait(bar, len(peers))

    s_in = [send(inp.at[rows(k * 2 + 1 - c)], par_in.at[k], partner) for k in range(2)]
    w1 = [send(ip.at[x], Wi.at[y, zl, c, x], d) for d in ypeer]

    def send_x(i):
        r = pl.ds(i * ti, ti)
        return [
            send(og.at[rows((1 - zl) * 2 + c, i, ti)], X.at[r, xcol(blk)], zlo),
            send(og.at[rows((1 - zl) * 2 + 1 - c, i, ti)], X.at[r, xcol(blk)], zlo_other),
        ]

    def send_wo(j):
        cs = pl.ds(j * wj, wj)
        return send(op.at[:, cs], Wo.at[xcol(blk), cs], zhi)

    xs = [send_x(0)]
    wos = [send_wo(0)]
    s_x = send(og.at[rows(zl * 2 + 1 - c)], X.at[:, xcol(blk)], partner)
    s_wo = send(op, Wo.at[xcol(blk)], partner)

    def packed(k):
        a, b = own_in[k], par_in[k]
        first = c == 0
        return jnp.concatenate([jnp.where(first, a, b), jnp.where(first, b, a)], axis=1)

    p_own = y * 2 + zl
    p_oth = y * 2 + 1 - zl
    for k in range(2):
        l_in[k].wait()
        s_in[k].wait_recv()
    pz[...] = packed(1 - zl)
    pzs = []
    for i in range(NI):
        r = pl.ds(i * ti, ti)
        pzs.append(send(pz.at[r], Y.at[r, ycol(p_own)], zlo))
    Y[:, ycol(p_own)] = packed(zl)
    yown = []
    for i in range(NI):
        r = pl.ds(i * ti, ti)
        yown.append([send(Y.at[r, ycol(p_own)], Y.at[r, ycol(p_own)], d) for d in ypeer])
    for i in range(1, NI):
        xs.append(send_x(i))

    l_wi.wait()
    for cp in w1:
        cp.wait_recv()
    w2 = send(Wi.at[:, zl, c, x], Wi.at[:, zl, c, x], zhi)
    for j in range(1, NJ):
        wos.append(send_wo(j))

    def send_w3(cls, j):
        cs = pl.ds(j * wj, wj)
        ref = Wi.at[:, cls, c, x, :, cs]
        return [send(ref, ref, d) for d in xpeer]

    w3a = [send_w3(zl, j) for j in range(NJ)]
    yrel = []
    for i in range(NI):
        r = pl.ds(i * ti, ti)
        pzs[i].wait_recv()
        yrel.append([send(Y.at[r, ycol(p_oth)], Y.at[r, ycol(p_oth)], d) for d in ypeer])
    w2.wait_recv()
    w3b = [send_w3(1 - zl, j) for j in range(NJ)]

    l_x.wait()
    l_wo.wait()
    s_x.wait_recv()
    s_wo.wait_recv()

    def forward(j):
        cs = pl.ds(j * wj, wj)
        wos[j].wait_recv()
        ref = Wo.at[xcol(oblk), cs]
        out = [send(ref, ref, partner)]
        for cp in w3a[j] + w3b[j]:
            cp.wait_recv()
        for zz in range(2):
            ref = Wi.at[:, zz, c, :, :, cs]
            out.append(send(ref, ref, partner))
        return out

    def block(i, j):
        r = pl.ds(pl.multiple_of(i * ti, ti), ti)
        cs = pl.ds(pl.multiple_of(j * wj, wj), wj)
        o = jnp.dot(X[r, :], Wo[:, cs], preferred_element_type=F32)
        wi = Wi[:, :, :, :, :, cs].reshape(Wo.shape[0], wj)
        n = jnp.dot(Y[r, :], wi, preferred_element_type=F32)
        s = jnp.sum(o * n, axis=0, keepdims=True)
        row = pl.ds(blk * 2 + (i * ti) // SEQ, 1)
        part[row, cs] = part[row, cs] + s

    def arrived(i):
        for cp in xs[i] + yown[i] + yrel[i]:
            cp.wait_recv()

    def compute(m):
        lax.fori_loop(0, m + 1, lambda j, u: (block(m, j), u)[1], 0)
        if m:
            lax.fori_loop(0, m, lambda i, u: (block(i, m), u)[1], 0)

    for m in range(NJ):
        fw = forward(m)
        if m:
            compute(m - 1)
        arrived(m)
        for cp in fw:
            cp.wait_recv()
    compute(NJ - 1)

    def tcol(k):
        return pl.ds(pl.multiple_of(k * 128, 128), 128)

    n_before = len(copies)
    r1 = [
        send(part.at[:, tcol((t + d) % 16)], r1buf.at[d], (dp, (t + d) % 16)) for d in range(1, 16)
    ]
    for cp in copies[:n_before]:
        cp.wait_send()
    total = part[:, tcol(t)]
    for cp in r1:
        cp.wait_recv()
    for d in range(1, 16):
        total = total + r1buf[d]
    own = total * F32(1.0 / math.sqrt(SEQ))
    feat_out[...] = own
    drow = pl.ds(pl.multiple_of(dp * 8, 8), 8)
    fall[drow, tcol(t)] = own
    r2 = [send(fall.at[drow, tcol(t)], fall.at[drow, tcol(t)], d) for d in dpeer]
    for cp in r2:
        cp.wait_recv()
    mine = fall.at[:, tcol(t)]
    r3 = [send(mine, mine, dev(x, zh, (y + d // 2) % 4, (zl + d % 2) % 2, c)) for d in range(1, 8)]
    r3p = send(mine, mine, partner)
    r4 = []
    for d in range(1, 8):
        r3[d - 1].wait_recv()
        ref = fall.at[:, tcol(((y - d // 2 + 4) % 4 * 2 + (zl + d % 2) % 2) * 2 + c)]
        r4.append(send(ref, ref, partner))
    r3p.wait_recv()
    for cp in r4:
        cp.wait_recv()
    f = fall[...]
    a = fall[:, tcol(t)]

    def halves(v):
        hi = v.astype(BF16)
        return hi, (v - hi.astype(F32)).astype(BF16)

    fh, fl = halves(f)
    ah, al = halves(a)
    g = lax.dot_general(
        jnp.concatenate([ah, ah, al], axis=0),
        jnp.concatenate([fh, fl, fh], axis=0),
        (((0,), (0,)), ((), ())),
        preferred_element_type=F32,
    )
    gram_out[...] = prev[...] + g * F32(1.0 / 64)
    for cp in copies[n_before:]:
        cp.wait_send()


def local(out_grads, inputs, out_proj, in_proj, prev_gram):
    tok = out_grads.shape[0] // 4
    width = out_proj.shape[1]
    return pl.pallas_call(
        kernel,
        out_shape=(
            jax.ShapeDtypeStruct((8, 128), F32),
            jax.ShapeDtypeStruct((128, width), F32),
        ),
        in_specs=[pl.BlockSpec(memory_space=pl.ANY)] * 4 + [pl.BlockSpec(memory_space=pltpu.VMEM)],
        out_specs=[pl.BlockSpec(memory_space=pltpu.VMEM)] * 2,
        scratch_shapes=[
            pltpu.VMEM((tok, 1024), BF16),
            pltpu.VMEM((tok, 1024), BF16),
            pltpu.VMEM((1024, width), BF16),
            pltpu.VMEM((4, 2, 2, 4, 16, width), BF16),
            pltpu.VMEM((2, tok, 64), BF16),
            pltpu.VMEM((2, tok, 64), BF16),
            pltpu.VMEM((tok, 128), BF16),
            pltpu.VMEM((8, width), F32),
            pltpu.VMEM((16, 8, 128), F32),
            pltpu.VMEM((64, width), F32),
            pltpu.SemaphoreType.DMA((8,)),
            pltpu.SemaphoreType.DMA((140,)),
            pltpu.SemaphoreType.DMA((140,)),
        ],
        compiler_params=pltpu.CompilerParams(
            collective_id=0, has_side_effects=True, vmem_limit_bytes=48 * 2**20
        ),
        name="features_gram",
    )(out_grads, inputs, out_proj, in_proj.reshape(4, 16, width), prev_gram)


def solution(mesh):
    return jax.shard_map(
        local,
        mesh=mesh,
        in_specs=(
            P("dp", "tensor"),
            P("dp", "tensor"),
            P("tensor", None),
            P("tensor", None),
            P("tensor", None),
        ),
        out_specs=(P("dp", "tensor"), P("tensor", None)),
        check_vma=False,
    )
```

```python
import math

import jax
import jax.numpy as jnp
from jax import lax
from jax.experimental import pallas as pl
from jax.experimental.pallas import tpu as pltpu
from jax.sharding import PartitionSpec as P

SEQ = 512
NI = 4
NJ = 4
F32 = jnp.float32
BF16 = jnp.bfloat16
MESH = pl.DeviceIdType.MESH


class Copy:
    def __init__(self, cp, remote):
        self.cp, self.remote, self.sent, self.got = cp, remote, not remote, False
        cp.start()

    def wait_recv(self):
        if self.got:
            return
        if self.remote:
            self.cp.wait_recv()
        else:
            self.cp.wait()
        self.got = True

    def wait_send(self):
        if not self.sent:
            self.cp.wait_send()
        self.sent = True


def kernel(
    og, inp, op, ip, prev, feat_out, gram_out, fall, X, Y, Wo, Wi, pk, pz, part, rbuf, lsem, ssem, rsem
):
    dp = lax.axis_index("dp")
    t = lax.axis_index("tensor")
    x, zh = dp // 2, dp % 2
    y, zl, c = t // 4, (t // 2) % 2, t % 2
    tok = og.shape[0] // 4
    width = op.shape[1]
    ti, wj = tok // NI, width // NJ

    def dev(x_, zh_, y_, zl_, c_):
        return (x_ * 2 + zh_, (y_ * 2 + zl_) * 2 + c_)

    partner = dev(x, zh, y, zl, 1 - c)
    zlo = dev(x, zh, y, 1 - zl, c)
    zlo_other = dev(x, zh, y, 1 - zl, 1 - c)
    zhi = dev(x, 1 - zh, y, 1 - zl, c)
    order = (1, 3, 2)
    zl_own, zl_oth = 0, 1
    ypeer = [dev(x, zh, (y + d) % 4, zl, c) for d in order]
    xdir = (1 + 2 * c, 3 - 2 * c)
    xpeer = [dev((x + d) % 4, zh, y, zl, c) for d in xdir]

    def shifted(dx, dz, sign):
        z_ = (zh * 2 + zl + 4 + sign * dz) % 4
        return ((x + 4 + sign * dx) % 4, z_ // 2, z_ % 2)

    steps = [(dx, dz) for dx in range(4) for dz in range(4) if dx or dz]
    steps.sort(key=lambda s: min(s[0], 4 - s[0]) + min(s[1], 4 - s[1]))

    def plane(s):
        x_, zh_, zl_ = shifted(*s, 1)
        return dev(x_, zh_, y, zl_, c)

    copies, locals_ = [], []

    def send(src, dst, device):
        k = len(copies)
        copies.append(
            Copy(
                pltpu.make_async_remote_copy(
                    src_ref=src, dst_ref=dst, send_sem=ssem.at[k], recv_sem=rsem.at[k],
                    device_id=device, device_id_type=MESH,
                ),
                True,
            )
        )
        return copies[-1]

    def local(src, dst):
        locals_.append(Copy(pltpu.make_async_copy(src, dst, lsem.at[len(locals_)]), False))
        return locals_[-1]

    blk = zl * 2 + c
    d_near, d_far = xdir[1], xdir[0]
    oblk = (1 - zl) * 2 + c
    p_own = y * 2 + zl
    p_oth = y * 2 + 1 - zl

    def rows(b, start=0, size=tok):
        return pl.ds(pl.multiple_of(b * tok + start, 128), size)

    def wrow(b):
        return pl.ds(pl.multiple_of(b * 256, 256), 256)

    def col(d):
        return (x + d) % 4

    def cols(d):
        return pl.ds(pl.multiple_of(col(d) * wj, wj), wj)

    def irow(core):
        return pl.ds(pl.multiple_of(core * 64, 64), 64)

    l_in = [local(inp.at[:, rows(k * 2 + c)], pk.at[k, irow(c)]) for k in range(2)]
    l_wi = local(ip.at[:, cols(0)], Wi.at[x, y, zl, c])
    part[...] = jnp.zeros_like(part)

    bar = pltpu.get_barrier_semaphore()
    peers = [partner, zlo_other] + ypeer + [plane(s) for s in steps]
    for d in peers:
        pl.semaphore_signal(bar, inc=1, device_id=d, device_id_type=MESH)
    pl.semaphore_wait(bar, len(peers))

    s_in = [
        send(inp.at[:, rows(k * 2 + 1 - c)], pk.at[k, irow(c)], partner) for k in (0, 1)
    ]
    w_own = ip.at[:, cols(0)]
    w_to = Wi.at[x, y, zl, c]
    w1 = [send(w_own, w_to, d) for d in ypeer]
    w2 = [send(w_own, w_to, zhi)]
    w3 = {}
    w3[zl_own, 0] = [send(w_own, w_to, d) for d in xpeer]

    def send_wo(d, start, size):
        r = pl.ds(start, size)
        to = pl.ds(pl.multiple_of(blk * 256 + start, 128), size)
        return send(op.at[r, cols(d)], Wo.at[col(d), to], zhi)

    def send_x(start, size):
        r = pl.ds(start, size)
        return [
            send(og.at[rows((1 - zl) * 2 + c, start, size)], X.at[blk, r], zlo),
            send(og.at[rows((1 - zl) * 2 + 1 - c, start, size)], X.at[blk, r], zlo_other),
        ]

    xs = [send_x(0, ti // 2)]
    wo_x = [send_wo(0, 0, 128)]

    for k in range(2):
        l_in[k].wait_recv()
        s_in[k].wait_recv()
    pzs = []
    for i in range(NI):
        r = pl.ds(i * ti, ti)
        pz[r, :] = pk[1 - zl, :, r].T
        pzs.append(send(pz.at[r], Y.at[p_own, r], zlo))
    xs[0] += send_x(ti // 2, ti // 2)
    for i in range(1, NI):
        xs.append(send_x(i * ti, ti))
    yown, yrel, yfar, d_wi = [], [], {}, {}

    def send_own(i):
        r = pl.ds(i * ti, ti)
        Y[p_own, r, :] = pk[zl, :, r].T
        yown.append([send(Y.at[p_own, r], Y.at[p_own, r], d) for d in ypeer[:2]])

    def pass_w1(k):
        w1[k].wait_recv()
        ref = Wi.at[x, (y + 4 - order[k]) % 4, zl, c]
        w2.append(send(ref, ref, zhi))
        w3[zl_own, k + 1] = [send(ref, ref, d) for d in xpeer]

    def pass_w2(k):
        w2[k].wait_recv()
        y_ = y if k == 0 else (y + 4 - order[k - 1]) % 4
        ref = Wi.at[x, y_, 1 - zl, c]
        w3[zl_oth, k] = [send(ref, ref, d) for d in xpeer]

    def relay(i):
        r = pl.ds(i * ti, ti)
        pzs[i].wait_recv()
        yrel.append([send(Y.at[p_oth, r], Y.at[p_oth, r], d) for d in ypeer[:2]])

    def pass_y(cps, cls, i):
        k, up = i % 2, (1, 3)[i % 2]
        cps[i][k].wait_recv()
        ref = Y.at[(y + 4 - up) % 4 * 2 + cls, pl.ds(i * ti, ti)]
        return send(ref, ref, ypeer[k])

    def own_far(i):
        yfar[0, i] = pass_y(yown, zl, i)

    def rel_far(i):
        yfar[1, i] = pass_y(yrel, 1 - zl, i)

    send_own(0)
    send_own(1)
    pass_w1(0)
    pass_w1(1)
    pass_w2(0)
    pass_w1(2)
    wo_x.append(send_wo(0, 128, 128))
    wo_2 = send_wo(2, 0, 256)
    wo_far = send_wo(d_far, 0, 256)
    s_wo = [send(op.at[:, cols(d)], Wo.at[col(d), wrow(blk)], partner) for d in range(NJ)]
    s_x = send(og.at[rows(zl * 2 + 1 - c)], X.at[blk], partner)
    l_x = local(og.at[rows(blk)], X.at[blk])
    l_wo = [local(op.at[:, cols(d)], Wo.at[col(d), wrow(blk)]) for d in range(NJ)]
    l_prev = local(prev, gram_out)
    relay(0)
    own_far(0)
    relay(1)
    pass_w2(1)
    own_far(1)
    pass_w2(2)
    rel_far(0)
    pass_w2(3)
    l_wi.wait_recv()
    ref = Wi.at[x, :, :, c]
    d_wi[0] = send(ref, ref, partner)
    rel_far(1)

    def pass_x(cls, k):
        for q in range(4):
            w3[cls, q][k].wait_recv()
        ref = Wi.at[(x + 4 - xdir[k]) % 4, :, (zl, 1 - zl)[cls], c]
        return send(ref, ref, xpeer[k])

    x_a = pass_x(zl_own, 1)
    send_own(2)
    send_own(3)
    relay(2)
    relay(3)
    for cp in wo_x:
        cp.wait_recv()
    ref = Wo.at[x, wrow(oblk)]
    d_wo = [send(ref, ref, partner)]
    x_b = pass_x(zl_oth, 0)
    wo_near = send(ref, ref, xpeer[0])

    def block(start, size, js):
        r = pl.ds(start, size)
        xv = jnp.concatenate([X[b, r, :] for b in range(4)], axis=1)
        yv = jnp.concatenate([Y[p, r, :] for p in range(8)], axis=1)
        wo = jnp.concatenate([Wo[j] for j in js], axis=1)
        wi = jnp.concatenate([Wi[j].reshape(Wo.shape[1], wj) for j in js], axis=1)
        o = jnp.dot(xv, wo, preferred_element_type=F32)
        n = jnp.dot(yv, wi, preferred_element_type=F32)
        s = jnp.sum(o * n, axis=0, keepdims=True)
        clip = start // SEQ
        for q, j in enumerate(js):
            for k in range(4):
                row = pl.ds(j * 4 + k, 1)
                at = q * wj + k * 128
                part[clip, row, :] = part[clip, row, :] + s[:, at : at + 128]

    def arrived(i):
        for cp in xs[i] + yown[i] + yrel[i] + [yfar[0, i], yfar[1, i]]:
            cp.wait_recv()

    def compute(start, size, first, step, count):
        def body(m, u):
            block(start, size, [(x + first + step * m) % 4])
            return u

        lax.fori_loop(0, count, body, 0)

    def compute_all(start, size):
        def body(m, u):
            block(start, size, [(x + 2 * m) % 4, (x + 2 * m + 1) % 4])
            return u

        lax.fori_loop(0, 2, body, 0)

    l_x.wait_recv()
    for cp in l_wo + [s_x] + s_wo:
        cp.wait_recv()
    arrived(0)
    d_wi[0].wait_recv()
    d_wo[0].wait_recv()
    compute(0, ti, 0, 1, 1)
    for q in range(4):
        for k in range(2):
            w3[zl_own, q][k].wait_recv()
            w3[zl_oth, q][k].wait_recv()
    for d in (1, 3):
        ref = Wi.at[col(d), :, :, c]
        d_wi[d] = send(ref, ref, partner)
    own_far(2)
    own_far(3)
    arrived(1)
    compute(ti, ti, 0, 1, 1)
    rel_far(2)
    rel_far(3)
    x_a.wait_recv()
    x_b.wait_recv()
    ref = Wi.at[col(2), :, :, c]
    d_wi[2] = send(ref, ref, partner)
    wo_2.wait_recv()
    ref = Wo.at[col(2), wrow(oblk)]
    d_wo.append(send(ref, ref, partner))
    d_wi[2].wait_recv()
    d_wo[1].wait_recv()
    compute(0, 2 * ti, 2, 1, 1)
    for cp, d in ((wo_far, d_far), (wo_near, d_near)):
        cp.wait_recv()
        ref = Wo.at[col(d), wrow(oblk)]
        d_wo.append(send(ref, ref, partner))
    arrived(2)
    compute(2 * ti, ti, 0, 2, 2)
    for k in range(2):
        d_wi[2 * k + 1].wait_recv()
        d_wo[2 + k].wait_recv()
    me = dp * 2 + zl

    def add_up(clip):
        return [
            send(part.at[clip], rbuf.at[clip, d - 1], dev(x, zh, (y + d) % 4, zl, c))
            for d in range(1, 4)
        ]

    def spread(clip, cps):
        for cp in cps:
            cp.wait_recv()
        own = (part[clip] + rbuf[clip, 0]) + (rbuf[clip, 1] + rbuf[clip, 2])
        fall[clip, me, c] = own * F32(1.0 / math.sqrt(SEQ))
        mine = fall.at[clip, me, c]
        return [send(mine, mine, plane(s)) for s in steps], [send(mine, mine, partner)]

    def hand_over(clip, cps, out):
        for s, cp in zip(steps, cps):
            cp.wait_recv()
            x_, zh_, zl_ = shifted(*s, -1)
            ref = fall.at[clip, (x_ * 2 + zh_) * 2 + zl_, c]
            out.append(send(ref, ref, partner))

    compute(0, 2 * ti, 1, 2, 2)
    main = list(copies)
    r1 = add_up(0)
    compute(2 * ti, ti, 1, 2, 2)
    r2, r3 = spread(0, r1)
    for cp in main:
        cp.wait_send()
    l_prev.wait_recv()
    arrived(3)
    compute_all(3 * ti, ti)
    r1b = add_up(1)
    hand_over(0, r2, r3)
    r2b, r3b = spread(1, r1b)
    for cp in copies:
        if not cp.sent and cp not in r2b and cp not in r3b:
            cp.wait_send()
    hand_over(1, r2b, r3b)
    for cp in r3 + r3b:
        cp.wait_recv()

    flat = fall.reshape(2 * 16 * 2 * 16, 128)

    def clips(j, lane):
        return flat[pl.ds(j * 4 + lane, 64, stride=16), :]

    def halves(v):
        hi = v.astype(BF16)
        return hi, (v - hi.astype(F32)).astype(BF16)

    ah, al = halves(clips(y, t % 4))
    a3 = jnp.concatenate([ah, ah, al], axis=0)
    for j in range(NJ):
        fh, fl = halves(jnp.concatenate([clips(j, lane) for lane in range(4)], axis=1))
        g = lax.dot_general(
            a3,
            jnp.concatenate([fh, fl, fh], axis=0),
            (((0,), (0,)), ((), ())),
            preferred_element_type=F32,
        )
        cs = pl.ds(j * wj, wj)
        gram_out[:, cs] = gram_out[:, cs] + g * F32(1.0 / 64)
    for k in range(8):
        row = ((k % 2 * 16 + dp * 2 + k // 4) * 2 + k // 2 % 2) * 16 + y * 4 + t % 4
        feat_out[k : k + 1, :] = flat[pl.ds(row, 1), :]
    for cp in copies:
        if not cp.sent:
            cp.wait_send()


def local(out_grads, inputs, out_proj, in_proj, prev_gram):
    tok = out_grads.shape[0] // 4
    width = out_proj.shape[1]
    wj = width // NJ
    vmem = pl.BlockSpec(memory_space=pltpu.VMEM)
    hbm = pl.BlockSpec(memory_space=pltpu.HBM)
    operands = (out_grads, inputs.T, out_proj, in_proj, prev_gram)
    return pl.pallas_call(
        kernel,
        out_shape=(
            jax.ShapeDtypeStruct((8, 128), F32),
            jax.ShapeDtypeStruct((128, width), F32),
        ),
        in_specs=[hbm] * 5,
        out_specs=[vmem] * 2,
        scratch_shapes=[
            pltpu.VMEM((2, 16, 2, 16, 128), F32),
            pltpu.VMEM((4, tok, 256), BF16),
            pltpu.VMEM((8, tok, 128), BF16),
            pltpu.VMEM((NJ, 1024, wj), BF16),
            pltpu.VMEM((NJ, 4, 2, 2, 64, wj), BF16),
            pltpu.VMEM((2, 128, tok), BF16),
            pltpu.VMEM((tok, 128), BF16),
            pltpu.VMEM((2, 16, 128), F32),
            pltpu.VMEM((2, 3, 16, 128), F32),
            pltpu.SemaphoreType.DMA((10,)),
            pltpu.SemaphoreType.DMA((160,)),
            pltpu.SemaphoreType.DMA((160,)),
        ],
        compiler_params=pltpu.CompilerParams(
            collective_id=0, has_side_effects=True, vmem_limit_bytes=40 * 2**20
        ),
        name="features_gram",
    )(*[pltpu.with_memory_space_constraint(a, pltpu.HBM) for a in operands])


def solution(mesh):
    return jax.shard_map(
        local,
        mesh=mesh,
        in_specs=(
            P("dp", "tensor"),
            P("dp", "tensor"),
            P("tensor", None),
            P("tensor", None),
            P("tensor", None),
        ),
        out_specs=(P("dp", "tensor"), P("tensor", None)),
        check_vma=False,
    )
```

```python
import math

import jax
import jax.numpy as jnp
from jax import lax
from jax.experimental import pallas as pl
from jax.experimental.pallas import tpu as pltpu
from jax.sharding import PartitionSpec as P

SEQ = 512
NI = 4
NJ = 4
F32 = jnp.float32
BF16 = jnp.bfloat16
MESH = pl.DeviceIdType.MESH


class Copy:
    def __init__(self, cp, remote):
        self.cp, self.remote, self.sent, self.got = cp, remote, not remote, False
        cp.start()

    def wait_recv(self):
        if self.got:
            return
        if self.remote:
            self.cp.wait_recv()
        else:
            self.cp.wait()
        self.got = True

    def wait_send(self):
        if not self.sent:
            self.cp.wait_send()
        self.sent = True


def kernel(
    og, inp, op, ip, prev, feat_out, gram_out, fall, X, Y, Wo, Wi, pk, pz, part, rbuf, lsem, ssem, rsem, word
):
    dp = lax.axis_index("dp")
    t = lax.axis_index("tensor")
    x, zh = dp // 2, dp % 2
    y, zl, c = t // 4, (t // 2) % 2, t % 2
    tok = og.shape[0] // 4
    width = op.shape[1]
    ti, wj = tok // NI, width // NJ

    def dev(x_, zh_, y_, zl_, c_):
        return (x_ * 2 + zh_, (y_ * 2 + zl_) * 2 + c_)

    partner = dev(x, zh, y, zl, 1 - c)
    zlo = dev(x, zh, y, 1 - zl, c)
    zlo_other = dev(x, zh, y, 1 - zl, 1 - c)
    zhi = dev(x, 1 - zh, y, 1 - zl, c)
    order = (1, 3, 2)
    zl_own, zl_oth = 0, 1
    ypeer = [dev(x, zh, (y + d) % 4, zl, c) for d in order]
    xdir = (1 + 2 * c, 3 - 2 * c)
    xpeer = [dev((x + d) % 4, zh, y, zl, c) for d in xdir]

    def shifted(dx, dz, sign):
        z_ = (zh * 2 + zl + 4 + sign * dz) % 4
        return ((x + 4 + sign * dx) % 4, z_ // 2, z_ % 2)

    steps = [(dx, dz) for dx in range(4) for dz in range(4) if dx or dz]
    steps.sort(key=lambda s: min(s[0], 4 - s[0]) + min(s[1], 4 - s[1]))

    def plane(s, core=c):
        x_, zh_, zl_ = shifted(*s, 1)
        return dev(x_, zh_, y, zl_, core)

    copies, locals_ = [], []

    def send(src, dst, device):
        k = len(copies)
        copies.append(
            Copy(
                pltpu.make_async_remote_copy(
                    src_ref=src, dst_ref=dst, send_sem=ssem.at[k], recv_sem=rsem.at[k],
                    device_id=device, device_id_type=MESH,
                ),
                True,
            )
        )
        return copies[-1]

    def local(src, dst):
        locals_.append(Copy(pltpu.make_async_copy(src, dst, lsem.at[len(locals_)]), False))
        return locals_[-1]

    blk = zl * 2 + c
    d_near, d_far = 3, 1
    xsides = [dev((x + d) % 4, zh, y, zl, c) for d in (1, 3)]
    oblk = (1 - zl) * 2 + c
    p_own = y * 2 + zl
    p_oth = y * 2 + 1 - zl

    def rows(b, start=0, size=tok):
        return pl.ds(pl.multiple_of(b * tok + start, 128), size)

    def wrow(b):
        return pl.ds(pl.multiple_of(b * 256, 256), 256)

    def col(d):
        return (x + d) % 4

    def cols(d):
        return pl.ds(pl.multiple_of(col(d) * wj, wj), wj)

    def irow(core):
        return pl.ds(pl.multiple_of(core * 64, 64), 64)

    l_in = [local(inp.at[:, rows(k * 2 + c)], pk.at[k, irow(c)]) for k in range(2)]
    l_wi = local(ip.at[:, cols(0)], Wi.at[x, y, zl, c])
    part[...] = jnp.zeros_like(part)

    bar = pltpu.get_barrier_semaphore()
    near = [partner] + [plane(s) for s in steps[:4]]
    peers = [zlo_other] + ypeer + near
    for d in peers:
        pl.semaphore_signal(bar, inc=1, device_id=d, device_id_type=MESH)
    pl.semaphore_wait(bar, len(peers))

    def pass_word(k):
        if k:
            pl.semaphore_wait(word.at[k - 1], len(near))
        if k < 4:
            for d in near:
                pl.semaphore_signal(word.at[k], inc=1, device_id=d, device_id_type=MESH)

    pass_word(0)

    s_in = [
        send(inp.at[:, rows(k * 2 + 1 - c)], pk.at[k, irow(c)], partner) for k in (0, 1)
    ]
    w_own = ip.at[:, cols(0)]
    w_to = Wi.at[x, y, zl, c]
    w1 = [send(w_own, w_to, d) for d in ypeer]
    w2 = [send(w_own, w_to, zhi)]
    w3 = {}
    w3[zl_own, 0] = [send(w_own, w_to, d) for d in xsides]

    def send_wo(d, start, size):
        r = pl.ds(start, size)
        to = pl.ds(pl.multiple_of(blk * 256 + start, 128), size)
        return send(op.at[r, cols(d)], Wo.at[col(d), to], zhi)

    def send_x(start, size):
        r = pl.ds(start, size)
        return [
            send(og.at[rows((1 - zl) * 2 + c, start, size)], X.at[blk, r], zlo),
            send(og.at[rows((1 - zl) * 2 + 1 - c, start, size)], X.at[blk, r], zlo_other),
        ]

    xs = [send_x(0, ti // 2)]
    wo_x = [send_wo(0, 0, 128)]

    for k in range(2):
        l_in[k].wait_recv()
        s_in[k].wait_recv()
    pzs = []
    for i in range(NI):
        r = pl.ds(i * ti, ti)
        pz[r, :] = pk[1 - zl, :, r].T
        pzs.append(send(pz.at[r], Y.at[p_own, r], zlo))
    xs[0] += send_x(ti // 2, ti // 2)
    for i in range(1, NI):
        xs.append(send_x(i * ti, ti))
    yown, yrel, yfar, d_wi = [], [], {}, {}

    def send_own(i):
        r = pl.ds(i * ti, ti)
        Y[p_own, r, :] = pk[zl, :, r].T
        yown.append([send(Y.at[p_own, r], Y.at[p_own, r], d) for d in ypeer[:2]])

    def pass_w1(k):
        w1[k].wait_recv()
        ref = Wi.at[x, (y + 4 - order[k]) % 4, zl, c]
        w2.append(send(ref, ref, zhi))
        w3[zl_own, k + 1] = [send(ref, ref, d) for d in xsides]

    def pass_w2(k):
        w2[k].wait_recv()
        y_ = y if k == 0 else (y + 4 - order[k - 1]) % 4
        ref = Wi.at[x, y_, 1 - zl, c]
        w3[zl_oth, k] = [send(ref, ref, d) for d in xpeer]

    def relay(i):
        r = pl.ds(i * ti, ti)
        pzs[i].wait_recv()
        yrel.append([send(Y.at[p_oth, r], Y.at[p_oth, r], d) for d in ypeer[:2]])

    def pass_y(cps, cls, i):
        k, up = i % 2, (1, 3)[i % 2]
        cps[i][k].wait_recv()
        ref = Y.at[(y + 4 - up) % 4 * 2 + cls, pl.ds(i * ti, ti)]
        return send(ref, ref, ypeer[k])

    def own_far(i):
        yfar[0, i] = pass_y(yown, zl, i)

    def rel_far(i):
        yfar[1, i] = pass_y(yrel, 1 - zl, i)

    send_own(0)
    send_own(1)
    pass_w1(0)
    pass_w1(1)
    pass_w2(0)
    pass_w1(2)
    wo_x.append(send_wo(0, 128, 128))
    wo_far = send_wo(d_far, 0, 256)
    wo_2 = send_wo(2, 0, 256)
    s_wo = [send(op.at[:, cols(d)], Wo.at[col(d), wrow(blk)], partner) for d in range(NJ)]
    s_x = send(og.at[rows(zl * 2 + 1 - c)], X.at[blk], partner)
    l_x = local(og.at[rows(blk)], X.at[blk])
    l_wo = [local(op.at[:, cols(d)], Wo.at[col(d), wrow(blk)]) for d in range(NJ)]
    l_prev = local(prev, gram_out)
    relay(0)
    own_far(0)
    relay(1)
    pass_w2(1)
    own_far(1)
    pass_w2(2)
    rel_far(0)
    pass_w2(3)
    l_wi.wait_recv()
    ref = Wi.at[x, :, :, c]
    d_wi[0] = send(ref, ref, partner)
    rel_far(1)

    def pass_x(cls, k, d, device):
        for q in range(4):
            w3[cls, q][k].wait_recv()
        ref = Wi.at[(x + 4 - d) % 4, :, (zl, 1 - zl)[cls], c]
        return send(ref, ref, device)

    x_a = pass_x(zl_own, 1, 3, xsides[1])
    send_own(2)
    send_own(3)
    relay(2)
    relay(3)
    pass_word(1)
    for cp in wo_x:
        cp.wait_recv()
    ref = Wo.at[x, wrow(oblk)]
    d_wo = [send(ref, ref, partner)]
    x_b = pass_x(zl_oth, 0, xdir[0], xpeer[0])
    wo_near = send(ref, ref, xsides[0])

    def block(start, size, js):
        r = pl.ds(start, size)
        xv = jnp.concatenate([X[b, r, :] for b in range(4)], axis=1)
        yv = jnp.concatenate([Y[p, r, :] for p in range(8)], axis=1)
        wo = jnp.concatenate([Wo[j] for j in js], axis=1)
        wi = jnp.concatenate([Wi[j].reshape(Wo.shape[1], wj) for j in js], axis=1)
        o = jnp.dot(xv, wo, preferred_element_type=F32)
        n = jnp.dot(yv, wi, preferred_element_type=F32)
        s = jnp.sum(o * n, axis=0, keepdims=True)
        clip = start // SEQ
        for q, j in enumerate(js):
            for k in range(4):
                row = pl.ds(j * 4 + k, 1)
                at = q * wj + k * 128
                part[clip, row, :] = part[clip, row, :] + s[:, at : at + 128]

    def arrived(i):
        for cp in xs[i] + yown[i] + yrel[i] + [yfar[0, i], yfar[1, i]]:
            cp.wait_recv()

    def compute(start, size, first, step, count):
        def body(m, u):
            block(start, size, [(x + first + step * m) % 4])
            return u

        lax.fori_loop(0, count, body, 0)

    def compute_all(start, size):
        def body(m, u):
            block(start, size, [(x + 2 * m) % 4, (x + 2 * m + 1) % 4])
            return u

        lax.fori_loop(0, 2, body, 0)

    l_x.wait_recv()
    for cp in l_wo + [s_x] + s_wo:
        cp.wait_recv()
    arrived(0)
    d_wi[0].wait_recv()
    d_wo[0].wait_recv()
    compute(0, ti, 0, 1, 1)
    for q in range(4):
        for k in range(2):
            w3[zl_own, q][k].wait_recv()
            w3[zl_oth, q][k].wait_recv()
    for d in (1, 3):
        ref = Wi.at[col(d), :, :, c]
        d_wi[d] = send(ref, ref, partner)
    own_far(2)
    own_far(3)
    pass_word(2)
    arrived(1)
    compute(ti, ti, 0, 1, 1)
    rel_far(2)
    rel_far(3)
    wo_far.wait_recv()
    ref = Wo.at[col(d_far), wrow(oblk)]
    d_wo.append(send(ref, ref, partner))
    for cp in (d_wi[1], d_wi[3], d_wo[1]):
        cp.wait_recv()
    pass_word(3)
    compute(0, 2 * ti, d_far, 1, 1)
    x_a.wait_recv()
    x_b.wait_recv()
    ref = Wi.at[col(2), :, :, c]
    d_wi[2] = send(ref, ref, partner)
    wo_2.wait_recv()
    ref = Wo.at[col(2), wrow(oblk)]
    d_wo.append(send(ref, ref, partner))
    arrived(2)
    compute(2 * ti, ti, 0, d_far, 2)
    d_wi[2].wait_recv()
    d_wo[2].wait_recv()
    pass_word(4)
    compute(0, 2 * ti, 2, 1, 1)
    wo_near.wait_recv()
    ref = Wo.at[col(d_near), wrow(oblk)]
    d_wo.append(send(ref, ref, partner))
    compute(2 * ti, ti, 2, 1, 1)
    d_wo[3].wait_recv()
    me = dp * 2 + zl

    def add_up(clip):
        return [
            send(part.at[clip], rbuf.at[clip, d - 1], dev(x, zh, (y + d) % 4, zl, c))
            for d in range(1, 4)
        ]

    def spread(clip, cps):
        for cp in cps:
            cp.wait_recv()
        own = (part[clip] + rbuf[clip, 0]) + (rbuf[clip, 1] + rbuf[clip, 2])
        fall[clip, me, c] = own * F32(1.0 / math.sqrt(SEQ))
        mine = fall.at[clip, me, c]
        out = [send(mine, mine, plane(s)) for s in steps[::-1]][::-1]
        both = [send(mine, mine, plane(s, 1 - c)) for s in steps[10:]] if clip else []
        return out, both + [send(mine, mine, partner)]

    def hand_over(clip, cps, out):
        for k, (s, cp) in enumerate(zip(steps, cps)):
            cp.wait_recv()
            if clip and k >= 10:
                continue
            x_, zh_, zl_ = shifted(*s, -1)
            ref = fall.at[clip, (x_ * 2 + zh_) * 2 + zl_, c]
            out.append(send(ref, ref, partner))

    compute(0, 2 * ti, d_near, 1, 1)
    main = list(copies)
    r1 = add_up(0)
    compute(2 * ti, ti, d_near, 1, 1)
    r2, r3 = spread(0, r1)
    for cp in main:
        cp.wait_send()
    l_prev.wait_recv()
    arrived(3)
    compute_all(3 * ti, ti)
    r1b = add_up(1)
    hand_over(0, r2, r3)
    r2b, r3b = spread(1, r1b)
    for cp in copies:
        if not cp.sent and cp not in r2b and cp not in r3b:
            cp.wait_send()
    hand_over(1, r2b, r3b)
    for cp in r3 + r3b:
        cp.wait_recv()

    flat = fall.reshape(2 * 16 * 2 * 16, 128)

    def clips(j, lane):
        return flat[pl.ds(j * 4 + lane, 64, stride=16), :]

    def halves(v):
        hi = v.astype(BF16)
        return hi, (v - hi.astype(F32)).astype(BF16)

    ah, al = halves(clips(y, t % 4))
    a3 = jnp.concatenate([ah, ah, al], axis=0)
    for j in range(NJ):
        fh, fl = halves(jnp.concatenate([clips(j, lane) for lane in range(4)], axis=1))
        g = lax.dot_general(
            a3,
            jnp.concatenate([fh, fl, fh], axis=0),
            (((0,), (0,)), ((), ())),
            preferred_element_type=F32,
        )
        cs = pl.ds(j * wj, wj)
        gram_out[:, cs] = gram_out[:, cs] + g * F32(1.0 / 64)
    for k in range(8):
        row = ((k % 2 * 16 + dp * 2 + k // 4) * 2 + k // 2 % 2) * 16 + y * 4 + t % 4
        feat_out[k : k + 1, :] = flat[pl.ds(row, 1), :]
    for cp in copies:
        if not cp.sent:
            cp.wait_send()


def local(out_grads, inputs, out_proj, in_proj, prev_gram):
    tok = out_grads.shape[0] // 4
    width = out_proj.shape[1]
    wj = width // NJ
    vmem = pl.BlockSpec(memory_space=pltpu.VMEM)
    hbm = pl.BlockSpec(memory_space=pltpu.HBM)
    operands = (out_grads, inputs.T, out_proj, in_proj, prev_gram)
    return pl.pallas_call(
        kernel,
        out_shape=(
            jax.ShapeDtypeStruct((8, 128), F32),
            jax.ShapeDtypeStruct((128, width), F32),
        ),
        in_specs=[hbm] * 5,
        out_specs=[vmem] * 2,
        scratch_shapes=[
            pltpu.VMEM((2, 16, 2, 16, 128), F32),
            pltpu.VMEM((4, tok, 256), BF16),
            pltpu.VMEM((8, tok, 128), BF16),
            pltpu.VMEM((NJ, 1024, wj), BF16),
            pltpu.VMEM((NJ, 4, 2, 2, 64, wj), BF16),
            pltpu.VMEM((2, 128, tok), BF16),
            pltpu.VMEM((tok, 128), BF16),
            pltpu.VMEM((2, 16, 128), F32),
            pltpu.VMEM((2, 3, 16, 128), F32),
            pltpu.SemaphoreType.DMA((10,)),
            pltpu.SemaphoreType.DMA((160,)),
            pltpu.SemaphoreType.DMA((160,)),
            pltpu.SemaphoreType.REGULAR((4,)),
        ],
        compiler_params=pltpu.CompilerParams(
            collective_id=0, has_side_effects=True, vmem_limit_bytes=40 * 2**20
        ),
        name="features_gram",
    )(*[pltpu.with_memory_space_constraint(a, pltpu.HBM) for a in operands])


def solution(mesh):
    return jax.shard_map(
        local,
        mesh=mesh,
        in_specs=(
            P("dp", "tensor"),
            P("dp", "tensor"),
            P("tensor", None),
            P("tensor", None),
            P("tensor", None),
        ),
        out_specs=(P("dp", "tensor"), P("tensor", None)),
        check_vma=False,
    )
```

```python
import math

import jax
import jax.numpy as jnp
from jax import lax
from jax.experimental import pallas as pl
from jax.experimental.pallas import tpu as pltpu
from jax.sharding import PartitionSpec as P

SEQ = 512
NI = 4
NJ = 4
F32 = jnp.float32
BF16 = jnp.bfloat16
MESH = pl.DeviceIdType.MESH


class Copy:
    def __init__(self, cp, remote):
        self.cp, self.remote, self.sent, self.got = cp, remote, not remote, False
        cp.start()

    def wait_recv(self):
        if self.got:
            return
        if self.remote:
            self.cp.wait_recv()
        else:
            self.cp.wait()
        self.got = True

    def wait_send(self):
        if not self.sent:
            self.cp.wait_send()
        self.sent = True


def kernel(
    og, inp, op, ip, prev, feat_out, gram_out, fall, X, Y, Wo, Wi, pk, pz, part, rbuf, lsem, ssem, rsem, word
):
    dp = lax.axis_index("dp")
    t = lax.axis_index("tensor")
    x, zh = dp // 2, dp % 2
    y, zl, c = t // 4, (t // 2) % 2, t % 2
    tok = og.shape[0] // 4
    width = op.shape[1]
    ti, wj = tok // NI, width // NJ

    def dev(x_, zh_, y_, zl_, c_):
        return (x_ * 2 + zh_, (y_ * 2 + zl_) * 2 + c_)

    partner = dev(x, zh, y, zl, 1 - c)
    zlo = dev(x, zh, y, 1 - zl, c)
    zlo_other = dev(x, zh, y, 1 - zl, 1 - c)
    zhi = dev(x, 1 - zh, y, 1 - zl, c)
    order = (1, 3, 2)
    zl_own, zl_oth = 0, 1
    ypeer = [dev(x, zh, (y + d) % 4, zl, c) for d in order]
    xdir = (1 + 2 * c, 3 - 2 * c)
    xpeer = [dev((x + d) % 4, zh, y, zl, c) for d in xdir]

    def shifted(dx, dz, sign):
        z_ = (zh * 2 + zl + 4 + sign * dz) % 4
        return ((x + 4 + sign * dx) % 4, z_ // 2, z_ % 2)

    steps = [(dx, dz) for dx in range(4) for dz in range(4) if dx or dz]
    steps.sort(key=lambda s: min(s[0], 4 - s[0]) + min(s[1], 4 - s[1]))

    def plane(s, core=c):
        x_, zh_, zl_ = shifted(*s, 1)
        return dev(x_, zh_, y, zl_, core)

    copies, locals_ = [], []

    def send(src, dst, device):
        k = len(copies)
        copies.append(
            Copy(
                pltpu.make_async_remote_copy(
                    src_ref=src, dst_ref=dst, send_sem=ssem.at[k], recv_sem=rsem.at[k],
                    device_id=device, device_id_type=MESH,
                ),
                True,
            )
        )
        return copies[-1]

    def local(src, dst):
        locals_.append(Copy(pltpu.make_async_copy(src, dst, lsem.at[len(locals_)]), False))
        return locals_[-1]

    blk = zl * 2 + c
    d_near, d_far = 3, 1
    xsides = [dev((x + d) % 4, zh, y, zl, c) for d in (1, 3)]
    oblk = (1 - zl) * 2 + c
    p_own = y * 2 + zl
    p_oth = y * 2 + 1 - zl

    def rows(b, start=0, size=tok):
        return pl.ds(pl.multiple_of(b * tok + start, 128), size)

    def wrow(b):
        return pl.ds(pl.multiple_of(b * 256, 256), 256)

    def col(d):
        return (x + d) % 4

    def cols(d):
        return pl.ds(pl.multiple_of(col(d) * wj, wj), wj)

    def irow(core):
        return pl.ds(pl.multiple_of(core * 64, 64), 64)

    l_wi = local(ip.at[:, cols(0)], Wi.at[x, y, zl, c])
    l_in = [local(inp.at[:, rows(k * 2 + c)], pk.at[k, irow(c)]) for k in range(2)]
    l_wo = {d: local(op.at[:, cols(d)], Wo.at[col(d), wrow(blk)]) for d in (0, 1, 2, 3)}
    part[...] = jnp.zeros_like(part)

    bar = pltpu.get_barrier_semaphore()
    near = [partner] + [plane(s) for s in steps[:4]]
    peers = [zlo_other] + ypeer + near
    for d in peers:
        pl.semaphore_signal(bar, inc=1, device_id=d, device_id_type=MESH)
    pl.semaphore_wait(bar, len(peers))

    def pass_word(k):
        if k:
            pl.semaphore_wait(word.at[k - 1], len(near))
        if k < 4:
            for d in near:
                pl.semaphore_signal(word.at[k], inc=1, device_id=d, device_id_type=MESH)

    pass_word(0)

    s_in = [
        send(inp.at[:, rows(k * 2 + 1 - c)], pk.at[k, irow(c)], partner) for k in (0, 1)
    ]
    l_wi.wait_recv()
    w_own = w_to = Wi.at[x, y, zl, c]
    w1 = [send(w_own, w_to, d) for d in ypeer]
    w2 = [send(w_own, w_to, zhi)]
    w3 = {}
    w3[zl_own, 0] = [send(w_own, w_to, d) for d in xsides]

    def send_wo(d, start, size):
        l_wo[d].wait_recv()
        ref = Wo.at[col(d), pl.ds(pl.multiple_of(blk * 256 + start, 128), size)]
        return send(ref, ref, zhi)

    def send_x(start, size):
        r = pl.ds(start, size)
        return [
            send(og.at[rows((1 - zl) * 2 + c, start, size)], X.at[blk, r], zlo),
            send(og.at[rows((1 - zl) * 2 + 1 - c, start, size)], X.at[blk, r], zlo_other),
        ]

    xs = [send_x(0, ti // 2)]
    wo_x = [send_wo(0, 0, 128)]

    for k in range(2):
        l_in[k].wait_recv()
        s_in[k].wait_recv()
    pzs = []
    for i in range(NI):
        r = pl.ds(i * ti, ti)
        pz[r, :] = pk[1 - zl, :, r].T
        pzs.append(send(pz.at[r], Y.at[p_own, r], zlo))
    xs[0] += send_x(ti // 2, ti // 2)
    for i in range(1, NI):
        xs.append(send_x(i * ti, ti))
    yown, yrel, yfar, d_wi = [], [], {}, {}

    def send_own(i):
        r = pl.ds(i * ti, ti)
        Y[p_own, r, :] = pk[zl, :, r].T
        yown.append([send(Y.at[p_own, r], Y.at[p_own, r], d) for d in ypeer[:2]])

    def pass_w1(k):
        w1[k].wait_recv()
        ref = Wi.at[x, (y + 4 - order[k]) % 4, zl, c]
        w2.append(send(ref, ref, zhi))
        w3[zl_own, k + 1] = [send(ref, ref, d) for d in xsides]

    def pass_w2(k):
        w2[k].wait_recv()
        y_ = y if k == 0 else (y + 4 - order[k - 1]) % 4
        ref = Wi.at[x, y_, 1 - zl, c]
        w3[zl_oth, k] = [send(ref, ref, d) for d in xpeer]

    def relay(i):
        r = pl.ds(i * ti, ti)
        pzs[i].wait_recv()
        yrel.append([send(Y.at[p_oth, r], Y.at[p_oth, r], d) for d in ypeer[:2]])

    def pass_y(cps, cls, i):
        k, up = i % 2, (1, 3)[i % 2]
        cps[i][k].wait_recv()
        ref = Y.at[(y + 4 - up) % 4 * 2 + cls, pl.ds(i * ti, ti)]
        return send(ref, ref, ypeer[k])

    def own_far(i):
        yfar[0, i] = pass_y(yown, zl, i)

    def rel_far(i):
        yfar[1, i] = pass_y(yrel, 1 - zl, i)

    send_own(0)
    send_own(1)
    pass_w1(0)
    pass_w1(1)
    pass_w2(0)
    pass_w1(2)
    wo_x.append(send_wo(0, 128, 128))
    wo_far = send_wo(d_far, 0, 256)
    wo_2 = send_wo(2, 0, 256)
    s_wo = []
    for d in range(NJ):
        l_wo[d].wait_recv()
        ref = Wo.at[col(d), wrow(blk)]
        s_wo.append(send(ref, ref, partner))
    s_x = send(og.at[rows(zl * 2 + 1 - c)], X.at[blk], partner)
    l_x = local(og.at[rows(blk)], X.at[blk])
    l_prev = local(prev, gram_out)
    relay(0)
    own_far(0)
    relay(1)
    pass_w2(1)
    own_far(1)
    pass_w2(2)
    rel_far(0)
    pass_w2(3)
    ref = Wi.at[x, :, :, c]
    d_wi[0] = send(ref, ref, partner)
    rel_far(1)

    def pass_x(cls, k, d, device):
        for q in range(4):
            w3[cls, q][k].wait_recv()
        ref = Wi.at[(x + 4 - d) % 4, :, (zl, 1 - zl)[cls], c]
        return send(ref, ref, device)

    x_a = pass_x(zl_own, 1, 3, xsides[1])
    send_own(2)
    send_own(3)
    relay(2)
    relay(3)
    pass_word(1)
    for cp in wo_x:
        cp.wait_recv()
    ref = Wo.at[x, wrow(oblk)]
    d_wo = [send(ref, ref, partner)]
    x_b = pass_x(zl_oth, 0, xdir[0], xpeer[0])
    wo_near = send(ref, ref, xsides[0])

    def block(start, size, js):
        r = pl.ds(start, size)
        xv = jnp.concatenate([X[b, r, :] for b in range(4)], axis=1)
        yv = jnp.concatenate([Y[p, r, :] for p in range(8)], axis=1)
        wo = jnp.concatenate([Wo[j] for j in js], axis=1)
        wi = jnp.concatenate([Wi[j].reshape(Wo.shape[1], wj) for j in js], axis=1)
        o = jnp.dot(xv, wo, preferred_element_type=F32)
        n = jnp.dot(yv, wi, preferred_element_type=F32)
        s = jnp.sum(o * n, axis=0, keepdims=True)
        clip = start // SEQ
        for q, j in enumerate(js):
            for k in range(4):
                row = pl.ds(j * 4 + k, 1)
                at = q * wj + k * 128
                part[clip, row, :] = part[clip, row, :] + s[:, at : at + 128]

    def arrived(i):
        for cp in xs[i] + yown[i] + yrel[i] + [yfar[0, i], yfar[1, i]]:
            cp.wait_recv()

    def compute(start, size, first, step, count):
        def body(m, u):
            block(start, size, [(x + first + step * m) % 4])
            return u

        lax.fori_loop(0, count, body, 0)

    def compute_pair(start, size, m):
        block(start, size, [(x + 2 * m) % 4, (x + 2 * m + 1) % 4])

    l_x.wait_recv()
    for cp in [s_x] + s_wo:
        cp.wait_recv()
    arrived(0)
    d_wi[0].wait_recv()
    d_wo[0].wait_recv()
    compute(0, ti, 0, 1, 1)
    for q in range(4):
        for k in range(2):
            w3[zl_own, q][k].wait_recv()
            w3[zl_oth, q][k].wait_recv()
    for d in (1, 3):
        ref = Wi.at[col(d), :, :, c]
        d_wi[d] = send(ref, ref, partner)
    own_far(2)
    own_far(3)
    pass_word(2)
    arrived(1)
    compute(ti, ti, 0, 1, 1)
    rel_far(2)
    rel_far(3)
    wo_far.wait_recv()
    ref = Wo.at[col(d_far), wrow(oblk)]
    d_wo.append(send(ref, ref, partner))
    for cp in (d_wi[1], d_wi[3], d_wo[1]):
        cp.wait_recv()
    pass_word(3)
    compute(0, 2 * ti, d_far, 1, 1)
    x_a.wait_recv()
    x_b.wait_recv()
    ref = Wi.at[col(2), :, :, c]
    d_wi[2] = send(ref, ref, partner)
    wo_2.wait_recv()
    ref = Wo.at[col(2), wrow(oblk)]
    d_wo.append(send(ref, ref, partner))
    arrived(2)
    compute(2 * ti, ti, 0, d_far, 2)
    d_wi[2].wait_recv()
    d_wo[2].wait_recv()
    pass_word(4)
    compute(0, 2 * ti, 2, 1, 1)
    wo_near.wait_recv()
    ref = Wo.at[col(d_near), wrow(oblk)]
    d_wo.append(send(ref, ref, partner))
    compute(2 * ti, ti, 2, 1, 1)
    d_wo[3].wait_recv()
    me = dp * 2 + zl

    def add_up(clip):
        return [
            send(part.at[clip], rbuf.at[clip, d - 1], dev(x, zh, (y + d) % 4, zl, c))
            for d in range(1, 4)
        ]

    def spread(clip, cps):
        for cp in cps:
            cp.wait_recv()
        own = (part[clip] + rbuf[clip, 0]) + (rbuf[clip, 1] + rbuf[clip, 2])
        fall[clip, me, c] = own * F32(1.0 / math.sqrt(SEQ))
        mine = fall.at[clip, me, c]
        out = [send(mine, mine, plane(s)) for s in steps[::-1]][::-1]
        both = [send(mine, mine, plane(s, 1 - c)) for s in steps[10:]] if clip else []
        return out, both + [send(mine, mine, partner)]

    def hand_over(clip, cps, out):
        for k, (s, cp) in enumerate(zip(steps, cps)):
            cp.wait_recv()
            if clip and k >= 10:
                continue
            x_, zh_, zl_ = shifted(*s, -1)
            ref = fall.at[clip, (x_ * 2 + zh_) * 2 + zl_, c]
            out.append(send(ref, ref, partner))

    compute(0, 2 * ti, d_near, 1, 1)
    main = list(copies)
    r1 = add_up(0)
    compute(2 * ti, ti, d_near, 1, 1)
    arrived(3)
    lax.fori_loop(0, 2, lambda m, u: (compute_pair(3 * ti, ti, m), u)[1], 0)
    r1b = add_up(1)
    r2, r3 = spread(0, r1)
    for cp in main:
        cp.wait_send()
    l_prev.wait_recv()
    r2b, r3b = spread(1, r1b)
    hand_over(0, r2, r3)
    hand_over(1, r2b, r3b)
    for cp in copies:
        if not cp.sent:
            cp.wait_send()
    for cp in r3 + r3b:
        cp.wait_recv()

    flat = fall.reshape(2 * 16 * 2 * 16, 128)

    def clips(j, lane):
        return flat[pl.ds(j * 4 + lane, 64, stride=16), :]

    def halves(v):
        hi = v.astype(BF16)
        return hi, (v - hi.astype(F32)).astype(BF16)

    ah, al = halves(clips(y, t % 4))
    a3 = jnp.concatenate([ah, ah, al], axis=0)
    for j in range(NJ):
        fh, fl = halves(jnp.concatenate([clips(j, lane) for lane in range(4)], axis=1))
        g = lax.dot_general(
            a3,
            jnp.concatenate([fh, fl, fh], axis=0),
            (((0,), (0,)), ((), ())),
            preferred_element_type=F32,
        )
        cs = pl.ds(j * wj, wj)
        gram_out[:, cs] = gram_out[:, cs] + g * F32(1.0 / 64)
    for k in range(8):
        row = ((k % 2 * 16 + dp * 2 + k // 4) * 2 + k // 2 % 2) * 16 + y * 4 + t % 4
        feat_out[k : k + 1, :] = flat[pl.ds(row, 1), :]
    for cp in copies:
        if not cp.sent:
            cp.wait_send()


def local(out_grads, inputs, out_proj, in_proj, prev_gram):
    tok = out_grads.shape[0] // 4
    width = out_proj.shape[1]
    wj = width // NJ
    vmem = pl.BlockSpec(memory_space=pltpu.VMEM)
    hbm = pl.BlockSpec(memory_space=pltpu.HBM)
    operands = (out_grads, inputs.T, out_proj, in_proj, prev_gram)
    return pl.pallas_call(
        kernel,
        out_shape=(
            jax.ShapeDtypeStruct((8, 128), F32),
            jax.ShapeDtypeStruct((128, width), F32),
        ),
        in_specs=[hbm] * 5,
        out_specs=[vmem] * 2,
        scratch_shapes=[
            pltpu.VMEM((2, 16, 2, 16, 128), F32),
            pltpu.VMEM((4, tok, 256), BF16),
            pltpu.VMEM((8, tok, 128), BF16),
            pltpu.VMEM((NJ, 1024, wj), BF16),
            pltpu.VMEM((NJ, 4, 2, 2, 64, wj), BF16),
            pltpu.VMEM((2, 128, tok), BF16),
            pltpu.VMEM((tok, 128), BF16),
            pltpu.VMEM((2, 16, 128), F32),
            pltpu.VMEM((2, 3, 16, 128), F32),
            pltpu.SemaphoreType.DMA((10,)),
            pltpu.SemaphoreType.DMA((160,)),
            pltpu.SemaphoreType.DMA((160,)),
            pltpu.SemaphoreType.REGULAR((4,)),
        ],
        compiler_params=pltpu.CompilerParams(
            collective_id=0, has_side_effects=True, vmem_limit_bytes=40 * 2**20
        ),
        name="features_gram",
    )(*[pltpu.with_memory_space_constraint(a, pltpu.HBM) for a in operands])


def solution(mesh):
    return jax.shard_map(
        local,
        mesh=mesh,
        in_specs=(
            P("dp", "tensor"),
            P("dp", "tensor"),
            P("tensor", None),
            P("tensor", None),
            P("tensor", None),
        ),
        out_specs=(P("dp", "tensor"), P("tensor", None)),
        check_vma=False,
    )
```

```python
import math

import jax
import jax.numpy as jnp
from jax import lax
from jax.experimental import pallas as pl
from jax.experimental.pallas import tpu as pltpu
from jax.sharding import PartitionSpec as P

SEQ = 512
NI = 4
NJ = 4
F32 = jnp.float32
BF16 = jnp.bfloat16
MESH = pl.DeviceIdType.MESH


class Copy:
    def __init__(self, cp, remote):
        self.cp, self.remote, self.sent, self.got = cp, remote, not remote, False
        cp.start()

    def wait_recv(self):
        if self.got:
            return
        if self.remote:
            self.cp.wait_recv()
        else:
            self.cp.wait()
        self.got = True

    def wait_send(self):
        if not self.sent:
            self.cp.wait_send()
        self.sent = True


def kernel(
    og, inp, op, ip, prev, feat_out, gram_out, fall, X, Y, Wo, Wi, pk, pz, part, rbuf, lsem, ssem, rsem, word
):
    dp = lax.axis_index("dp")
    t = lax.axis_index("tensor")
    x, zh = dp // 2, dp % 2
    y, zl, c = t // 4, (t // 2) % 2, t % 2
    tok = og.shape[0] // 4
    width = op.shape[1]
    ti, wj = tok // NI, width // NJ

    def dev(x_, zh_, y_, zl_, c_):
        return (x_ * 2 + zh_, (y_ * 2 + zl_) * 2 + c_)

    partner = dev(x, zh, y, zl, 1 - c)
    zlo = dev(x, zh, y, 1 - zl, c)
    zlo_other = dev(x, zh, y, 1 - zl, 1 - c)
    zhi = dev(x, 1 - zh, y, 1 - zl, c)
    order = (1, 3, 2)
    zl_own, zl_oth = 0, 1
    ypeer = [dev(x, zh, (y + d) % 4, zl, c) for d in order]
    xdir = (1 + 2 * c, 3 - 2 * c)
    xpeer = [dev((x + d) % 4, zh, y, zl, c) for d in xdir]

    def shifted(dx, dz, sign):
        z_ = (zh * 2 + zl + 4 + sign * dz) % 4
        return ((x + 4 + sign * dx) % 4, z_ // 2, z_ % 2)

    steps = [(dx, dz) for dx in range(4) for dz in range(4) if dx or dz]
    steps.sort(key=lambda s: min(s[0], 4 - s[0]) + min(s[1], 4 - s[1]))

    def plane(s, core=c):
        x_, zh_, zl_ = shifted(*s, 1)
        return dev(x_, zh_, y, zl_, core)

    copies, locals_ = [], []

    def send(src, dst, device):
        k = len(copies)
        copies.append(
            Copy(
                pltpu.make_async_remote_copy(
                    src_ref=src, dst_ref=dst, send_sem=ssem.at[k], recv_sem=rsem.at[k],
                    device_id=device, device_id_type=MESH,
                ),
                True,
            )
        )
        return copies[-1]

    def local(src, dst):
        locals_.append(Copy(pltpu.make_async_copy(src, dst, lsem.at[len(locals_)]), False))
        return locals_[-1]

    blk = zl * 2 + c
    d_near, d_far = 3, 1
    xsides = [dev((x + d) % 4, zh, y, zl, c) for d in (1, 3)]
    oblk = (1 - zl) * 2 + c
    p_own = y * 2 + zl
    p_oth = y * 2 + 1 - zl

    def rows(b, start=0, size=tok):
        return pl.ds(pl.multiple_of(b * tok + start, 128), size)

    def wrow(b):
        return pl.ds(pl.multiple_of(b * 256, 256), 256)

    def col(d):
        return (x + d) % 4

    def cols(d):
        return pl.ds(pl.multiple_of(col(d) * wj, wj), wj)

    def irow(core):
        return pl.ds(pl.multiple_of(core * 64, 64), 64)

    l_wi = local(ip.at[:, cols(0)], Wi.at[x, y, zl, c])
    l_in = [local(inp.at[:, rows(k * 2 + c)], pk.at[k, irow(c)]) for k in range(2)]
    l_wo = {d: local(op.at[:, cols(d)], Wo.at[col(d), wrow(blk)]) for d in (0, 1, 2, 3)}
    part[...] = jnp.zeros_like(part)

    bar = pltpu.get_barrier_semaphore()
    near = [partner] + [plane(s) for s in steps[:4]]
    peers = [zlo_other] + ypeer + near
    for d in peers:
        pl.semaphore_signal(bar, inc=1, device_id=d, device_id_type=MESH)
    pl.semaphore_wait(bar, len(peers))

    def pass_word(k):
        if k:
            pl.semaphore_wait(word.at[k - 1], len(near))
        if k < 4:
            for d in near:
                pl.semaphore_signal(word.at[k], inc=1, device_id=d, device_id_type=MESH)

    pass_word(0)

    s_in = [
        send(inp.at[:, rows(k * 2 + 1 - c)], pk.at[k, irow(c)], partner) for k in (0, 1)
    ]
    l_wi.wait_recv()
    w_own = w_to = Wi.at[x, y, zl, c]
    w1 = [send(w_own, w_to, d) for d in ypeer]
    w2 = [send(w_own, w_to, zhi)]
    w3 = {}
    w3[zl_own, 0] = [send(w_own, w_to, d) for d in xsides]

    def send_wo(d, start, size):
        l_wo[d].wait_recv()
        ref = Wo.at[col(d), pl.ds(pl.multiple_of(blk * 256 + start, 128), size)]
        return send(ref, ref, zhi)

    def send_x(start, size):
        r = pl.ds(start, size)
        return [
            send(og.at[rows((1 - zl) * 2 + c, start, size)], X.at[blk, r], zlo),
            send(og.at[rows((1 - zl) * 2 + 1 - c, start, size)], X.at[blk, r], zlo_other),
        ]

    xs = [send_x(0, ti // 2)]
    wo_x = [send_wo(0, 0, 128)]

    for k in range(2):
        l_in[k].wait_recv()
        s_in[k].wait_recv()
    pzs = []
    for i in range(NI):
        r = pl.ds(i * ti, ti)
        pz[r, :] = pk[1 - zl, :, r].T
        pzs.append(send(pz.at[r], Y.at[p_own, r], zlo))
    xs[0] += send_x(ti // 2, ti // 2)
    for i in range(1, NI):
        xs.append(send_x(i * ti, ti))
    yown, yrel, yfar, d_wi = [], [], {}, {}

    def send_own(i):
        r = pl.ds(i * ti, ti)
        Y[p_own, r, :] = pk[zl, :, r].T
        yown.append([send(Y.at[p_own, r], Y.at[p_own, r], d) for d in ypeer[:2]])

    def pass_w1(k):
        w1[k].wait_recv()
        ref = Wi.at[x, (y + 4 - order[k]) % 4, zl, c]
        w2.append(send(ref, ref, zhi))
        w3[zl_own, k + 1] = [send(ref, ref, d) for d in xsides]

    def pass_w2(k):
        w2[k].wait_recv()
        y_ = y if k == 0 else (y + 4 - order[k - 1]) % 4
        ref = Wi.at[x, y_, 1 - zl, c]
        w3[zl_oth, k] = [send(ref, ref, d) for d in xpeer]

    def relay(i):
        r = pl.ds(i * ti, ti)
        pzs[i].wait_recv()
        yrel.append([send(Y.at[p_oth, r], Y.at[p_oth, r], d) for d in ypeer[:2]])

    def pass_y(cps, cls, i):
        k, up = i % 2, (1, 3)[i % 2]
        cps[i][k].wait_recv()
        ref = Y.at[(y + 4 - up) % 4 * 2 + cls, pl.ds(i * ti, ti)]
        return send(ref, ref, ypeer[k])

    def own_far(i):
        yfar[0, i] = pass_y(yown, zl, i)

    def rel_far(i):
        yfar[1, i] = pass_y(yrel, 1 - zl, i)

    send_own(0)
    send_own(1)
    pass_w1(0)
    pass_w1(1)
    pass_w2(0)
    pass_w1(2)
    wo_x.append(send_wo(0, 128, 128))
    wo_far = send_wo(d_far, 0, 256)
    wo_2 = send_wo(2, 0, 256)
    s_wo = []
    for d in range(NJ):
        l_wo[d].wait_recv()
        ref = Wo.at[col(d), wrow(blk)]
        s_wo.append(send(ref, ref, partner))
    s_x = send(og.at[rows(zl * 2 + 1 - c)], X.at[blk], partner)
    l_x = local(og.at[rows(blk)], X.at[blk])
    l_prev = local(prev, gram_out)
    relay(0)
    own_far(0)
    relay(1)
    pass_w2(1)
    own_far(1)
    pass_w2(2)
    rel_far(0)
    pass_w2(3)
    ref = Wi.at[x, :, :, c]
    d_wi[0] = send(ref, ref, partner)
    rel_far(1)

    def pass_x(cls, k, d, device):
        for q in range(4):
            w3[cls, q][k].wait_recv()
        ref = Wi.at[(x + 4 - d) % 4, :, (zl, 1 - zl)[cls], c]
        return send(ref, ref, device)

    x_a = pass_x(zl_own, 1, 3, xsides[1])
    send_own(2)
    send_own(3)
    relay(2)
    relay(3)
    pass_word(1)
    for cp in wo_x:
        cp.wait_recv()
    ref = Wo.at[x, wrow(oblk)]
    d_wo = [send(ref, ref, partner)]
    x_b = pass_x(zl_oth, 0, xdir[0], xpeer[0])
    wo_near = send(ref, ref, xsides[0])

    def block(start, size, js):
        r = pl.ds(start, size)
        xv = jnp.concatenate([X[b, r, :] for b in range(4)], axis=1)
        yv = jnp.concatenate([Y[p, r, :] for p in range(8)], axis=1)
        wo = jnp.concatenate([Wo[j] for j in js], axis=1)
        wi = jnp.concatenate([Wi[j].reshape(Wo.shape[1], wj) for j in js], axis=1)
        o = jnp.dot(xv, wo, preferred_element_type=F32)
        n = jnp.dot(yv, wi, preferred_element_type=F32)
        s = jnp.sum(o * n, axis=0, keepdims=True)
        clip = start // SEQ
        for q, j in enumerate(js):
            for k in range(4):
                row = pl.ds(j * 4 + k, 1)
                at = q * wj + k * 128
                part[clip, row, :] = part[clip, row, :] + s[:, at : at + 128]

    def arrived(i):
        for cp in xs[i] + yown[i] + yrel[i] + [yfar[0, i], yfar[1, i]]:
            cp.wait_recv()

    def compute(start, size, first, step, count):
        def body(m, u):
            block(start, size, [(x + first + step * m) % 4])
            return u

        lax.fori_loop(0, count, body, 0)

    def compute_pair(start, size, m):
        block(start, size, [(x + 2 * m) % 4, (x + 2 * m + 1) % 4])

    l_x.wait_recv()
    for cp in [s_x] + s_wo:
        cp.wait_recv()
    arrived(0)
    d_wi[0].wait_recv()
    d_wo[0].wait_recv()
    compute(0, ti, 0, 1, 1)
    for q in range(4):
        for k in range(2):
            w3[zl_own, q][k].wait_recv()
            w3[zl_oth, q][k].wait_recv()
    for d in (1, 3):
        ref = Wi.at[col(d), :, :, c]
        d_wi[d] = send(ref, ref, partner)
    own_far(2)
    own_far(3)
    pass_word(2)
    arrived(1)
    compute(ti, ti, 0, 1, 1)
    rel_far(2)
    rel_far(3)
    wo_far.wait_recv()
    ref = Wo.at[col(d_far), wrow(oblk)]
    d_wo.append(send(ref, ref, partner))
    for cp in (d_wi[1], d_wi[3], d_wo[1]):
        cp.wait_recv()
    pass_word(3)
    compute(0, 2 * ti, d_far, 1, 1)
    x_a.wait_recv()
    x_b.wait_recv()
    ref = Wi.at[col(2), :, :, c]
    d_wi[2] = send(ref, ref, partner)
    wo_2.wait_recv()
    ref = Wo.at[col(2), wrow(oblk)]
    d_wo.append(send(ref, ref, partner))
    arrived(2)
    compute(2 * ti, ti, 0, d_far, 2)
    d_wi[2].wait_recv()
    d_wo[2].wait_recv()
    pass_word(4)
    wo_near.wait_recv()
    ref = Wo.at[col(d_near), wrow(oblk)]
    d_wo.append(send(ref, ref, partner))
    compute(0, 2 * ti, 2, 1, 1)
    compute(2 * ti, ti, 2, 1, 1)
    d_wo[3].wait_recv()
    me = dp * 2 + zl

    def add_up(clip):
        return [
            send(part.at[clip], rbuf.at[clip, d - 1], dev(x, zh, (y + d) % 4, zl, c))
            for d in range(1, 4)
        ]

    def spread(clip, cps):
        for cp in cps:
            cp.wait_recv()
        own = (part[clip] + rbuf[clip, 0]) + (rbuf[clip, 1] + rbuf[clip, 2])
        fall[clip, me, c] = own * F32(1.0 / math.sqrt(SEQ))
        mine = fall.at[clip, me, c]
        out = [send(mine, mine, plane(s)) for s in steps[::-1]][::-1]
        both = [send(mine, mine, plane(s, 1 - c)) for s in steps[10:]] if clip else []
        return out, both + [send(mine, mine, partner)]

    def hand_over(clip, cps, out):
        for k, (s, cp) in enumerate(zip(steps, cps)):
            cp.wait_recv()
            if clip and k >= 10:
                continue
            x_, zh_, zl_ = shifted(*s, -1)
            ref = fall.at[clip, (x_ * 2 + zh_) * 2 + zl_, c]
            out.append(send(ref, ref, partner))

    compute(0, 2 * ti, d_near, 1, 1)
    main = list(copies)
    r1 = add_up(0)
    compute(2 * ti, ti, d_near, 1, 1)
    arrived(3)
    lax.fori_loop(0, 2, lambda m, u: (compute_pair(3 * ti, ti, m), u)[1], 0)
    r1b = add_up(1)
    r2, r3 = spread(0, r1)
    for cp in main:
        cp.wait_send()
    l_prev.wait_recv()
    r2b, r3b = spread(1, r1b)
    hand_over(0, r2, r3)
    hand_over(1, r2b, r3b)
    for cp in copies:
        if not cp.sent:
            cp.wait_send()
    for cp in r3 + r3b:
        cp.wait_recv()

    flat = fall.reshape(2 * 16 * 2 * 16, 128)

    def clips(j, lane):
        return flat[pl.ds(j * 4 + lane, 64, stride=16), :]

    def halves(v):
        hi = v.astype(BF16)
        return hi, (v - hi.astype(F32)).astype(BF16)

    ah, al = halves(clips(y, t % 4))
    a3 = jnp.concatenate([ah, ah, al], axis=0)
    for j in range(NJ):
        fh, fl = halves(jnp.concatenate([clips(j, lane) for lane in range(4)], axis=1))
        g = lax.dot_general(
            a3,
            jnp.concatenate([fh, fl, fh], axis=0),
            (((0,), (0,)), ((), ())),
            preferred_element_type=F32,
        )
        cs = pl.ds(j * wj, wj)
        gram_out[:, cs] = gram_out[:, cs] + g * F32(1.0 / 64)
    for k in range(8):
        row = ((k % 2 * 16 + dp * 2 + k // 4) * 2 + k // 2 % 2) * 16 + y * 4 + t % 4
        feat_out[k : k + 1, :] = flat[pl.ds(row, 1), :]
    for cp in copies:
        if not cp.sent:
            cp.wait_send()


def local(out_grads, inputs, out_proj, in_proj, prev_gram):
    tok = out_grads.shape[0] // 4
    width = out_proj.shape[1]
    wj = width // NJ
    vmem = pl.BlockSpec(memory_space=pltpu.VMEM)
    hbm = pl.BlockSpec(memory_space=pltpu.HBM)
    operands = (out_grads, inputs.T, out_proj, in_proj, prev_gram)
    return pl.pallas_call(
        kernel,
        out_shape=(
            jax.ShapeDtypeStruct((8, 128), F32),
            jax.ShapeDtypeStruct((128, width), F32),
        ),
        in_specs=[hbm] * 5,
        out_specs=[vmem] * 2,
        scratch_shapes=[
            pltpu.VMEM((2, 16, 2, 16, 128), F32),
            pltpu.VMEM((4, tok, 256), BF16),
            pltpu.VMEM((8, tok, 128), BF16),
            pltpu.VMEM((NJ, 1024, wj), BF16),
            pltpu.VMEM((NJ, 4, 2, 2, 64, wj), BF16),
            pltpu.VMEM((2, 128, tok), BF16),
            pltpu.VMEM((tok, 128), BF16),
            pltpu.VMEM((2, 16, 128), F32),
            pltpu.VMEM((2, 3, 16, 128), F32),
            pltpu.SemaphoreType.DMA((10,)),
            pltpu.SemaphoreType.DMA((160,)),
            pltpu.SemaphoreType.DMA((160,)),
            pltpu.SemaphoreType.REGULAR((4,)),
        ],
        compiler_params=pltpu.CompilerParams(
            collective_id=0, has_side_effects=True, vmem_limit_bytes=40 * 2**20
        ),
        name="features_gram",
    )(*[pltpu.with_memory_space_constraint(a, pltpu.HBM) for a in operands])


def solution(mesh):
    return jax.shard_map(
        local,
        mesh=mesh,
        in_specs=(
            P("dp", "tensor"),
            P("dp", "tensor"),
            P("tensor", None),
            P("tensor", None),
            P("tensor", None),
        ),
        out_specs=(P("dp", "tensor"), P("tensor", None)),
        check_vma=False,
    )
```

```python
import math

import jax
import jax.numpy as jnp
from jax import lax
from jax.experimental import pallas as pl
from jax.experimental.pallas import tpu as pltpu
from jax.sharding import PartitionSpec as P

SEQ = 512
NI = 4
NJ = 4
F32 = jnp.float32
BF16 = jnp.bfloat16
MESH = pl.DeviceIdType.MESH


class Copy:
    def __init__(self, cp, remote):
        self.cp, self.remote, self.sent, self.got = cp, remote, not remote, False
        cp.start()

    def wait_recv(self):
        if self.got:
            return
        if self.remote:
            self.cp.wait_recv()
        else:
            self.cp.wait()
        self.got = True

    def wait_send(self):
        if not self.sent:
            self.cp.wait_send()
        self.sent = True


def kernel(
    og, inp, op, ip, prev, feat_out, gram_out, fall, X, Y, Wo, Wi, pk, pz, part, rbuf, lsem, ssem, rsem, word
):
    dp = lax.axis_index("dp")
    t = lax.axis_index("tensor")
    x, zh = dp // 2, dp % 2
    y, zl, c = t // 4, (t // 2) % 2, t % 2
    tok = og.shape[0] // 4
    width = op.shape[1]
    ti, wj = tok // NI, width // NJ

    def dev(x_, zh_, y_, zl_, c_):
        return (x_ * 2 + zh_, (y_ * 2 + zl_) * 2 + c_)

    partner = dev(x, zh, y, zl, 1 - c)
    zlo = dev(x, zh, y, 1 - zl, c)
    zlo_other = dev(x, zh, y, 1 - zl, 1 - c)
    zhi = dev(x, 1 - zh, y, 1 - zl, c)
    order = (1, 3, 2)
    zl_own, zl_oth = 0, 1
    ypeer = [dev(x, zh, (y + d) % 4, zl, c) for d in order]
    xdir = (1 + 2 * c, 3 - 2 * c)
    xpeer = [dev((x + d) % 4, zh, y, zl, c) for d in xdir]

    def shifted(dx, dz, sign):
        z_ = (zh * 2 + zl + 4 + sign * dz) % 4
        return ((x + 4 + sign * dx) % 4, z_ // 2, z_ % 2)

    steps = [(dx, dz) for dx in range(4) for dz in range(4) if dx or dz]
    steps.sort(key=lambda s: min(s[0], 4 - s[0]) + min(s[1], 4 - s[1]))

    def plane(s, core=c):
        x_, zh_, zl_ = shifted(*s, 1)
        return dev(x_, zh_, y, zl_, core)

    copies, locals_ = [], []

    def send(src, dst, device):
        k = len(copies)
        copies.append(
            Copy(
                pltpu.make_async_remote_copy(
                    src_ref=src, dst_ref=dst, send_sem=ssem.at[k], recv_sem=rsem.at[k],
                    device_id=device, device_id_type=MESH,
                ),
                True,
            )
        )
        return copies[-1]

    def local(src, dst):
        locals_.append(Copy(pltpu.make_async_copy(src, dst, lsem.at[len(locals_)]), False))
        return locals_[-1]

    blk = zl * 2 + c
    d_near, d_far = 3, 1
    xsides = [dev((x + d) % 4, zh, y, zl, c) for d in (1, 3)]
    oblk = (1 - zl) * 2 + c
    p_own = y * 2 + zl
    p_oth = y * 2 + 1 - zl

    def rows(b, start=0, size=tok):
        return pl.ds(pl.multiple_of(b * tok + start, 128), size)

    def wrow(b):
        return pl.ds(pl.multiple_of(b * 256, 256), 256)

    def col(d):
        return (x + d) % 4

    def cols(d):
        return pl.ds(pl.multiple_of(col(d) * wj, wj), wj)

    def irow(core):
        return pl.ds(pl.multiple_of(core * 64, 64), 64)

    l_wi = local(ip.at[:, cols(0)], Wi.at[x, y, zl, c])
    l_in = [local(inp.at[:, rows(k * 2 + c)], pk.at[k, irow(c)]) for k in range(2)]
    l_wo = {d: local(op.at[:, cols(d)], Wo.at[col(d), wrow(blk)]) for d in (0, 1, 2, 3)}
    part[...] = jnp.zeros_like(part)

    bar = pltpu.get_barrier_semaphore()
    near = [partner] + [plane(s) for s in steps[:4]]
    peers = [zlo_other] + ypeer + near
    for d in peers:
        pl.semaphore_signal(bar, inc=1, device_id=d, device_id_type=MESH)
    pl.semaphore_wait(bar, len(peers))

    def pass_word(k):
        if k:
            pl.semaphore_wait(word.at[k - 1], len(near))
        if k < 4:
            for d in near:
                pl.semaphore_signal(word.at[k], inc=1, device_id=d, device_id_type=MESH)

    pass_word(0)

    s_in = [
        send(inp.at[:, rows(k * 2 + 1 - c)], pk.at[k, irow(c)], partner) for k in (0, 1)
    ]
    l_wi.wait_recv()
    w_own = w_to = Wi.at[x, y, zl, c]
    w1 = [send(w_own, w_to, d) for d in ypeer]
    w2 = [send(w_own, w_to, zhi)]
    w3 = {}
    w3[zl_own, 0] = [send(w_own, w_to, d) for d in xsides]

    def send_wo(d, start, size):
        l_wo[d].wait_recv()
        ref = Wo.at[col(d), pl.ds(pl.multiple_of(blk * 256 + start, 128), size)]
        return send(ref, ref, zhi)

    def send_x(start, size):
        r = pl.ds(start, size)
        return [
            send(og.at[rows((1 - zl) * 2 + c, start, size)], X.at[blk, r], zlo),
            send(og.at[rows((1 - zl) * 2 + 1 - c, start, size)], X.at[blk, r], zlo_other),
        ]

    xs = [send_x(0, ti // 2)]
    wo_x = [send_wo(0, 0, 128)]

    for k in range(2):
        l_in[k].wait_recv()
        s_in[k].wait_recv()
    pzs = []
    for i in range(NI):
        r = pl.ds(i * ti, ti)
        pz[r, :] = pk[1 - zl, :, r].T
        pzs.append(send(pz.at[r], Y.at[p_own, r], zlo))
    xs[0] += send_x(ti // 2, ti // 2)
    for i in range(1, NI):
        xs.append(send_x(i * ti, ti))
    yown, yrel, yfar, d_wi = [], [], {}, {}

    def send_own(i):
        r = pl.ds(i * ti, ti)
        Y[p_own, r, :] = pk[zl, :, r].T
        yown.append([send(Y.at[p_own, r], Y.at[p_own, r], d) for d in ypeer[:2]])

    def pass_w1(k):
        w1[k].wait_recv()
        ref = Wi.at[x, (y + 4 - order[k]) % 4, zl, c]
        w2.append(send(ref, ref, zhi))
        w3[zl_own, k + 1] = [send(ref, ref, d) for d in xsides]

    def pass_w2(k):
        w2[k].wait_recv()
        y_ = y if k == 0 else (y + 4 - order[k - 1]) % 4
        ref = Wi.at[x, y_, 1 - zl, c]
        w3[zl_oth, k] = [send(ref, ref, d) for d in xpeer]

    def relay(i):
        r = pl.ds(i * ti, ti)
        pzs[i].wait_recv()
        yrel.append([send(Y.at[p_oth, r], Y.at[p_oth, r], d) for d in ypeer[:2]])

    def pass_y(cps, cls, i):
        k, up = i % 2, (1, 3)[i % 2]
        cps[i][k].wait_recv()
        ref = Y.at[(y + 4 - up) % 4 * 2 + cls, pl.ds(i * ti, ti)]
        return send(ref, ref, ypeer[k])

    def own_far(i):
        yfar[0, i] = pass_y(yown, zl, i)

    def rel_far(i):
        yfar[1, i] = pass_y(yrel, 1 - zl, i)

    send_own(0)
    send_own(1)
    pass_w1(0)
    pass_w1(1)
    pass_w2(0)
    pass_w1(2)
    wo_x.append(send_wo(0, 128, 128))
    wo_far = send_wo(d_far, 0, 256)
    wo_2 = send_wo(2, 0, 256)
    s_wo = []
    for d in range(NJ):
        l_wo[d].wait_recv()
        ref = Wo.at[col(d), wrow(blk)]
        s_wo.append(send(ref, ref, partner))
    s_x = send(og.at[rows(zl * 2 + 1 - c)], X.at[blk], partner)
    l_x = local(og.at[rows(blk)], X.at[blk])
    l_prev = local(prev, gram_out)
    relay(0)
    own_far(0)
    relay(1)
    pass_w2(1)
    own_far(1)
    pass_w2(2)
    rel_far(0)
    pass_w2(3)
    ref = Wi.at[x, :, :, c]
    d_wi[0] = send(ref, ref, partner)
    rel_far(1)

    def pass_x(cls, k, d, device):
        for q in range(4):
            w3[cls, q][k].wait_recv()
        ref = Wi.at[(x + 4 - d) % 4, :, (zl, 1 - zl)[cls], c]
        return send(ref, ref, device)

    x_a = pass_x(zl_own, 1, 3, xsides[1])
    send_own(2)
    send_own(3)
    relay(2)
    relay(3)
    pass_word(1)
    for cp in wo_x:
        cp.wait_recv()
    ref = Wo.at[x, wrow(oblk)]
    d_wo = [send(ref, ref, partner)]
    x_b = pass_x(zl_oth, 0, xdir[0], xpeer[0])
    wo_near = send(ref, ref, xsides[0])

    def block(start, size, js):
        r = pl.ds(start, size)
        xv = jnp.concatenate([X[b, r, :] for b in range(4)], axis=1)
        yv = jnp.concatenate([Y[p, r, :] for p in range(8)], axis=1)
        wo = jnp.concatenate([Wo[j] for j in js], axis=1)
        wi = jnp.concatenate([Wi[j].reshape(Wo.shape[1], wj) for j in js], axis=1)
        o = jnp.dot(xv, wo, preferred_element_type=F32)
        n = jnp.dot(yv, wi, preferred_element_type=F32)
        s = jnp.sum(o * n, axis=0, keepdims=True)
        clip = start // SEQ
        for q, j in enumerate(js):
            for k in range(4):
                row = pl.ds(j * 4 + k, 1)
                at = q * wj + k * 128
                part[clip, row, :] = part[clip, row, :] + s[:, at : at + 128]

    def arrived(i):
        for cp in xs[i] + yown[i] + yrel[i] + [yfar[0, i], yfar[1, i]]:
            cp.wait_recv()

    def compute(start, size, first, step, count):
        def body(m, u):
            block(start, size, [(x + first + step * m) % 4])
            return u

        lax.fori_loop(0, count, body, 0)

    def compute_pair(start, size, m):
        block(start, size, [(x + 2 * m) % 4, (x + 2 * m + 1) % 4])

    l_x.wait_recv()
    for cp in [s_x] + s_wo:
        cp.wait_recv()
    arrived(0)
    d_wi[0].wait_recv()
    d_wo[0].wait_recv()
    compute(0, ti, 0, 1, 1)
    for q in range(4):
        for k in range(2):
            w3[zl_own, q][k].wait_recv()
            w3[zl_oth, q][k].wait_recv()
    for d in (1, 3):
        ref = Wi.at[col(d), :, :, c]
        d_wi[d] = send(ref, ref, partner)
    own_far(2)
    own_far(3)
    pass_word(2)
    arrived(1)
    compute(ti, ti, 0, 1, 1)
    rel_far(2)
    rel_far(3)
    wo_far.wait_recv()
    ref = Wo.at[col(d_far), wrow(oblk)]
    d_wo.append(send(ref, ref, partner))
    for cp in (d_wi[1], d_wi[3], d_wo[1]):
        cp.wait_recv()
    pass_word(3)
    compute(0, 2 * ti, d_far, 1, 1)
    x_a.wait_recv()
    x_b.wait_recv()
    ref = Wi.at[col(2), :, :, c]
    d_wi[2] = send(ref, ref, partner)
    wo_2.wait_recv()
    ref = Wo.at[col(2), wrow(oblk)]
    d_wo.append(send(ref, ref, partner))
    arrived(2)
    compute(2 * ti, ti, 0, d_far, 2)
    d_wi[2].wait_recv()
    d_wo[2].wait_recv()
    pass_word(4)
    wo_near.wait_recv()
    ref = Wo.at[col(d_near), wrow(oblk)]
    d_wo.append(send(ref, ref, partner))
    compute(0, 2 * ti, 2, 1, 1)
    compute(2 * ti, ti, 2, 1, 1)
    d_wo[3].wait_recv()
    me = dp * 2 + zl

    def add_up(clip):
        return [
            send(part.at[clip], rbuf.at[clip, d - 1], dev(x, zh, (y + d) % 4, zl, c))
            for d in range(1, 4)
        ]

    def spread(clip, cps):
        for cp in cps:
            cp.wait_recv()
        own = (part[clip] + rbuf[clip, 0]) + (rbuf[clip, 1] + rbuf[clip, 2])
        fall[clip, me, c] = own * F32(1.0 / math.sqrt(SEQ))
        mine = fall.at[clip, me, c]
        out = [send(mine, mine, plane(s)) for s in steps[::-1]][::-1]
        both = [send(mine, mine, plane(s, 1 - c)) for s in steps[4:]]
        return out, both + [send(mine, mine, partner)]

    def hand_over(clip, cps, out):
        for k, (s, cp) in enumerate(zip(steps, cps)):
            cp.wait_recv()
            if k >= 4:
                continue
            x_, zh_, zl_ = shifted(*s, -1)
            ref = fall.at[clip, (x_ * 2 + zh_) * 2 + zl_, c]
            out.append(send(ref, ref, partner))

    compute(0, 2 * ti, d_near, 1, 1)
    main = list(copies)
    r1 = add_up(0)
    compute(2 * ti, ti, d_near, 1, 1)
    arrived(3)
    lax.fori_loop(0, 2, lambda m, u: (compute_pair(3 * ti, ti, m), u)[1], 0)
    r1b = add_up(1)
    r2, r3 = spread(0, r1)
    for cp in main:
        cp.wait_send()
    l_prev.wait_recv()
    r2b, r3b = spread(1, r1b)
    hand_over(0, r2, r3)
    hand_over(1, r2b, r3b)
    for cp in copies:
        if not cp.sent:
            cp.wait_send()
    for cp in r3 + r3b:
        cp.wait_recv()

    flat = fall.reshape(2 * 16 * 2 * 16, 128)

    def clips(j, lane):
        return flat[pl.ds(j * 4 + lane, 64, stride=16), :]

    def halves(v):
        hi = v.astype(BF16)
        return hi, (v - hi.astype(F32)).astype(BF16)

    ah, al = halves(clips(y, t % 4))
    a3 = jnp.concatenate([ah, ah, al], axis=0)
    for j in range(NJ):
        fh, fl = halves(jnp.concatenate([clips(j, lane) for lane in range(4)], axis=1))
        g = lax.dot_general(
            a3,
            jnp.concatenate([fh, fl, fh], axis=0),
            (((0,), (0,)), ((), ())),
            preferred_element_type=F32,
        )
        cs = pl.ds(j * wj, wj)
        gram_out[:, cs] = gram_out[:, cs] + g * F32(1.0 / 64)
    for k in range(8):
        row = ((k % 2 * 16 + dp * 2 + k // 4) * 2 + k // 2 % 2) * 16 + y * 4 + t % 4
        feat_out[k : k + 1, :] = flat[pl.ds(row, 1), :]
    for cp in copies:
        if not cp.sent:
            cp.wait_send()


def local(out_grads, inputs, out_proj, in_proj, prev_gram):
    tok = out_grads.shape[0] // 4
    width = out_proj.shape[1]
    wj = width // NJ
    vmem = pl.BlockSpec(memory_space=pltpu.VMEM)
    hbm = pl.BlockSpec(memory_space=pltpu.HBM)
    operands = (out_grads, inputs.T, out_proj, in_proj, prev_gram)
    return pl.pallas_call(
        kernel,
        out_shape=(
            jax.ShapeDtypeStruct((8, 128), F32),
            jax.ShapeDtypeStruct((128, width), F32),
        ),
        in_specs=[hbm] * 5,
        out_specs=[vmem] * 2,
        scratch_shapes=[
            pltpu.VMEM((2, 16, 2, 16, 128), F32),
            pltpu.VMEM((4, tok, 256), BF16),
            pltpu.VMEM((8, tok, 128), BF16),
            pltpu.VMEM((NJ, 1024, wj), BF16),
            pltpu.VMEM((NJ, 4, 2, 2, 64, wj), BF16),
            pltpu.VMEM((2, 128, tok), BF16),
            pltpu.VMEM((tok, 128), BF16),
            pltpu.VMEM((2, 16, 128), F32),
            pltpu.VMEM((2, 3, 16, 128), F32),
            pltpu.SemaphoreType.DMA((10,)),
            pltpu.SemaphoreType.DMA((160,)),
            pltpu.SemaphoreType.DMA((160,)),
            pltpu.SemaphoreType.REGULAR((4,)),
        ],
        compiler_params=pltpu.CompilerParams(
            collective_id=0, has_side_effects=True, vmem_limit_bytes=40 * 2**20
        ),
        name="features_gram",
    )(*[pltpu.with_memory_space_constraint(a, pltpu.HBM) for a in operands])


def solution(mesh):
    return jax.shard_map(
        local,
        mesh=mesh,
        in_specs=(
            P("dp", "tensor"),
            P("dp", "tensor"),
            P("tensor", None),
            P("tensor", None),
            P("tensor", None),
        ),
        out_specs=(P("dp", "tensor"), P("tensor", None)),
        check_vma=False,
    )
```
